128 devices in a mesh: gx: 16 (over z, x), gy: 4 (over y), af: 2 (over core).
Axes of the slice: x: 4, y: 4, z: 4, core: 2. Of those that a mesh axis runs over, the one named last changes fastest.
Arguments:
- fields: float32 [6, 512, 64, 256], P(None, 'gx', 'gy', 'af'), may hold values from -6 to 6
- polarization: float32 [2, 3, 512, 64, 256], P(None, None, 'gx', 'gy', 'af'), may hold values from -2 to 2
- material: int32 [512, 64, 256], P('gx', 'gy', 'af'), may hold values from 0 to 3
- eps_inf: float32 [4], replicated, may hold values from 1 to 4
- pole_strength: float32 [4], replicated, may hold values from 0.5 to 3
- pole_freq: float32 [4], replicated, may hold values from 0.4 to 1.2
- damping: float32 [4], replicated, may hold values from 0.05 to 1
- owner: int32 [4, 2, 64, 1], P('gy', 'af'), may hold values from 0 to 15; in each aligned block of 64 rows (0 to 63, 64 to 127, ..., all dimensions but the last counted through in order) at most 8 rows name the same one
Outputs:
- fields_next: float32 [6, 512, 64, 256], P(None, 'gx', 'gy', 'af')
- polarization_next: float32 [2, 3, 512, 64, 256], P(None, None, 'gx', 'gy', 'af')
- surface_spectra: float32 [16, 4, 2, 8, 64, 128], P('gx', 'gy', 'af')
- far_field: float32 [8, 4096], P(None, ('gx', 'gy', 'af'))
The draws below stay inside these ranges and needn't reach their ends.
Inputs may be any that keep to these rules, and one draw needn't show every extreme that they name: `owner`: within the rows of one tile (aligned blocks of 64 rows) no gx index owns more than 8 rows, and some tile reaches 8.
All inputs are finite; a program needn't handle non-finite values.
Results may differ from the reference program's by a relative error of at most 0.0002.
Values sent between devices are 32-bit elements; how exact they have to be, the bound alone decides.
A program may use at most 128 MiB of HBM per device.

```python
import math
import jax
import jax.numpy as jnp
import numpy as np
from jax import lax

CY = 16
CZ = 128
STEPS = 8
NF = 32
NANG = 128
NMAT = 4
NX = 512
NY = 64
NZ = 256
SLOTS = 8
MONITOR_X = 496
N_GX = 16
N_GY = 4
N_AF = 2


def plant(entries, own_key, smallest, top_value):
    longest = entries.shape.index(max(entries.shape))
    spots = []
    for shift in (0, 1):
        where = [jax.random.randint(jax.random.fold_in(own_key, axis), (), 0, length) for axis, length in enumerate(entries.shape)]
        where[longest] = (where[longest] + shift) % entries.shape[longest]
        spots.append(tuple(where))
    return entries.at[spots[0]].set(smallest).at[spots[1]].set(top_value)


def steps_of(rng, shape, split, low, high):
    factor_of, own = 1.0, jax.random.fold_in(rng, 6)
    for axis_at, blocks in split:
        heights = jnp.exp(jax.random.uniform(jax.random.fold_in(own, axis_at), (blocks,), jnp.float32, low / len(split), high / len(split)))
        factor_of = factor_of * jnp.repeat(heights, shape[axis_at] // blocks).reshape([-1 if axis == axis_at else 1 for axis in range(len(shape))])
    return factor_of


def assign_block(key, own, number, rows, amount, top, bound, skew):
    sequence = jax.random.permutation(key, amount)
    packed, usual = load_shares(amount, rows * top, bound, skew, True), load_shares(amount, rows * top, bound, skew, False)
    places = jnp.arange(amount)

    def named(lengths, rotation):
        used = int((lengths > 0).sum())
        fixed = max(1, used // 4)
        shifted = fixed + (places - fixed + rotation * (used - fixed)) % max(1, amount - fixed)
        return jnp.zeros((amount,), jnp.int32).at[sequence[jnp.where(places < fixed, places, shifted)]].set(jnp.asarray(lengths, jnp.int32))

    lengths = jnp.where(number % 4 == 0, named(packed, number // 4), named(usual, number - number // 4 - 1))
    mixed = jax.random.permutation(jax.random.fold_in(own, 3), amount)
    source_of, sink = mixed[0:amount // 2 * 2:2], mixed[1:amount // 2 * 2:2]
    room = jnp.minimum(lengths[source_of] - 1, bound - lengths[sink]) // 2
    room = jnp.where((source_of == sequence[0]) | (sink == sequence[0]) | (lengths[sink] == 0), 0, jnp.maximum(room, 0))
    shifted = jax.random.randint(jax.random.fold_in(own, 4), (amount // 2,), 0, 1 << 20) % (room + 1)
    lengths = lengths.at[source_of].add(-shifted).at[sink].add(shifted)
    items = jnp.searchsorted(jnp.cumsum(lengths), jnp.arange(rows * top), side="right").astype(jnp.int32)
    table = items.reshape(top, rows).T
    table = table[jax.random.permutation(jax.random.fold_in(own, 1), rows)]
    rotation = jax.random.randint(jax.random.fold_in(own, 2), (rows, 1), 0, top)
    return jnp.take_along_axis(table, (jnp.arange(top)[None, :] + rotation) % top, axis=1)


def load_shares(number_of, total, most, skew, full):
    portions = [(1 << 20) // math.isqrt(rank ** skew) + 1 for rank in range(1, number_of + 1)]
    largest = most if full else min(most, max(-(-total // number_of), total * portions[0] // sum(portions)))
    least = 1 if total - largest >= number_of - 1 else 0
    holding, rest = [largest] + [least] * (number_of - 1), total - largest - least * (number_of - 1)
    while rest > 0:
        candidates = [i for i in range(1, number_of) if holding[i] < largest] or [i for i in range(1, number_of) if holding[i] < most]
        pool, remaining = sum([portions[i] for i in candidates]), rest
        for i in candidates:
            extra = min(most - holding[i], max(1, remaining * portions[i] // pool), rest)
            holding[i] = holding[i] + extra
            rest = rest - extra
    return np.array(holding)


def scatter_about(own_key, dims, spread, limit, pieces=(), kind=jnp.bfloat16):
    array = jax.random.normal(own_key, dims, jnp.float32) * spread
    if len(pieces) > 0:
        array = steps_of(own_key, dims, pieces, -0.22, 0.18) * array
    return jnp.clip(array, min=-limit, max=limit).astype(kind)


def setup_inputs(seed: int = 0) -> dict:
    key_list = jax.random.split(jax.random.key(seed), 9)
    fields = scatter_about(key_list[0], (6, NX, NY, NZ), 1.0, 6.0, ((1, 16), (2, 4), (3, 2)), jnp.float32)
    polarization = scatter_about(key_list[1], (2, 3, NX, NY, NZ), 0.3, 2.0, ((2, 16), (3, 4), (4, 2)), jnp.float32)
    material = plant(jax.random.randint(key_list[2], (NX, NY, NZ), 0, NMAT), jax.random.fold_in(key_list[2], 1), 0, NMAT - 1).astype(jnp.int32)
    eps_inf = jnp.clip(jax.random.uniform(key_list[3], (NMAT,), jnp.float32, 1.0, 4.0), 1.0, 4.0)
    pole_strength = jnp.clip(jax.random.uniform(key_list[4], (NMAT,), jnp.float32, 0.5, 3.0), 0.5, 3.0)
    pole_freq = jnp.clip(jax.random.uniform(key_list[5], (NMAT,), jnp.float32, 0.4, 1.2), 0.4, 1.2)
    damping = jnp.clip(jnp.exp(jax.random.uniform(key_list[6], (NMAT,), jnp.float32, math.log(0.05), math.log(1.0))), 0.05, 1.0)
    owner_keys = jax.random.split(jax.random.fold_in(key_list[7], 1), N_GY * N_AF * (4 * CY) // (4 * CY))
    owner_turns = jax.random.permutation(jax.random.fold_in(key_list[7], 3), N_GY * N_AF * (4 * CY) // (4 * CY))
    owner = jax.vmap(lambda own, number: assign_block(jax.random.fold_in(key_list[7], 2), own, number, 4 * CY, N_GX, 1, SLOTS, 2))(owner_keys, owner_turns).reshape((N_GY, N_AF, 4 * CY, 1))
    return {"fields": fields, "polarization": polarization, "material": material, "eps_inf": eps_inf, "pole_strength": pole_strength, "pole_freq": pole_freq, "damping": damping, "owner": owner}


step_size = 0.5
HIGH = lax.Precision.HIGHEST

def coefficient_fields(material, eps_inf, pole_strength, pole_freq, damping):
    turning = pole_freq * step_size
    half_loss = damping * (0.5 * step_size)
    denominator = 1.0 + half_loss
    tables = [(2.0 - turning * turning) / denominator, -(1.0 - half_loss) / denominator, pole_strength * turning * turning / denominator, 1.0 / eps_inf]
    fields_out = []
    for table_row in tables:
        values = jnp.zeros(material.shape, jnp.float32)
        for material_id in range(NMAT):
            values = jnp.where(material == material_id, table_row[material_id], values)
        fields_out.append(values)
    return fields_out

def frequencies():
    return 0.25 + 1.5 * jnp.arange(NF, dtype=jnp.float32) / NF

def time_table():
    phases = (jnp.arange(STEPS, dtype=jnp.float32) + 1.0) * step_size
    phases = phases[:, None] * frequencies()[None, :]
    return jnp.concatenate([jnp.cos(phases), -jnp.sin(phases)], axis=1) / STEPS

def directions():
    angles = jnp.arange(NANG, dtype=jnp.float32)
    bearing = 2.0 * math.pi * angles / NANG
    radius = 0.25 + 0.7 * (angles + 0.5) / NANG
    return (radius * jnp.cos(bearing), radius * jnp.sin(bearing))

def slot_table(owner_rows, owner_count, slot_count):
    one_hot = (owner_rows[..., None] == jnp.arange(owner_count, dtype=jnp.int32)).astype(jnp.int32)
    slot_rank = lax.optimization_barrier(jnp.sum((jnp.cumsum(one_hot, axis=-2) - 1) * one_hot, axis=-1))
    chosen = (slot_rank[..., None] == jnp.arange(slot_count, dtype=jnp.int32)).astype(jnp.int32)
    picked = one_hot[..., :, :, None] * chosen[..., :, None, :]
    return jnp.moveaxis(picked, -3, -1).astype(jnp.float32)

def ahead(values, spatial_dim):
    widths = [(0, 0)] * 3
    widths[spatial_dim] = (0, 1)
    return jnp.diff(jnp.pad(values, widths), axis=spatial_dim)

def behind(values, spatial_dim):
    widths = [(0, 0)] * 3
    widths[spatial_dim] = (1, 0)
    return jnp.diff(jnp.pad(values, widths), axis=spatial_dim)

def reference(fields, polarization, material, eps_inf, pole_strength, pole_freq, damping, owner):
    keep_rate, back_rate, drive_rate, inverse_eps = coefficient_fields(material, eps_inf, pole_strength, pole_freq, damping)
    time_weights = time_table()
    state = fields
    current = polarization[0]
    previous = polarization[1]
    spectra = jnp.zeros((2 * NF, 4, NY, NZ), jnp.float32)
    for step_number in range(STEPS):
        electric_x, electric_y, electric_z = (state[0], state[1], state[2])
        magnetic_x = state[3] - step_size * (ahead(electric_z, 1) - ahead(electric_y, 2))
        magnetic_y = state[4] - step_size * (ahead(electric_x, 2) - ahead(electric_z, 0))
        magnetic_z = state[5] - step_size * (ahead(electric_y, 0) - ahead(electric_x, 1))
        curl_x = behind(magnetic_z, 1) - behind(magnetic_y, 2)
        curl_y = behind(magnetic_x, 2) - behind(magnetic_z, 0)
        curl_z = behind(magnetic_y, 0) - behind(magnetic_x, 1)
        curl = jnp.stack([curl_x, curl_y, curl_z])
        electric = state[0:3]
        updated = keep_rate * current + back_rate * previous + drive_rate * electric
        electric = electric + inverse_eps * (step_size * curl - (updated - current))
        previous = current
        current = updated
        state = jnp.concatenate([electric, jnp.stack([magnetic_x, magnetic_y, magnetic_z])])
        samples = jnp.stack([state[1, MONITOR_X], state[2, MONITOR_X], state[4, MONITOR_X], state[5, MONITOR_X]])
        spectra = spectra + time_weights[step_number][:, None, None, None] * samples[None]
    blocks = spectra.reshape(2 * NF, 4, N_GY, CY, N_AF, CZ)
    blocks = jnp.transpose(blocks, (2, 4, 1, 3, 0, 5)).reshape(N_GY, N_AF, 4 * CY, 2 * NF, CZ)
    picked = slot_table(owner.reshape(N_GY, N_AF, 4 * CY), N_GX, SLOTS)
    routed = jnp.einsum('gaosr,garkz->ogaskz', picked, blocks, precision=HIGH)
    omegas = frequencies()
    along_y, along_z = directions()
    real_part = spectra[:NF]
    imag_part = spectra[NF:]
    z_phase = omegas[:, None, None] * along_z[None, None, :] * jnp.arange(NZ, dtype=jnp.float32)[None, :, None]
    cos_z = jnp.cos(z_phase)
    sin_z = jnp.sin(z_phase)
    inner_real = jnp.einsum('fcyz,fza->fcya', real_part, cos_z, precision=HIGH) - jnp.einsum('fcyz,fza->fcya', imag_part, sin_z, precision=HIGH)
    inner_imag = jnp.einsum('fcyz,fza->fcya', real_part, sin_z, precision=HIGH) + jnp.einsum('fcyz,fza->fcya', imag_part, cos_z, precision=HIGH)
    y_phase = omegas[:, None, None] * along_y[None, None, :] * jnp.arange(NY, dtype=jnp.float32)[None, :, None]
    cos_y = jnp.cos(y_phase)
    sin_y = jnp.sin(y_phase)
    far_real = jnp.einsum('fcya,fya->cfa', inner_real, cos_y, precision=HIGH) - jnp.einsum('fcya,fya->cfa', inner_imag, sin_y, precision=HIGH)
    far_imag = jnp.einsum('fcya,fya->cfa', inner_real, sin_y, precision=HIGH) + jnp.einsum('fcya,fya->cfa', inner_imag, cos_y, precision=HIGH)
    far_scale = 1.0 / math.sqrt(NY * NZ)
    far_field = jnp.stack([far_real, far_imag], axis=1).reshape(8, NF * NANG) * far_scale
    return (state, jnp.stack([current, previous]), routed, far_field)
```

```python
import functools
import math

import jax
import jax.numpy as jnp
import numpy as np
from jax import lax
from jax.experimental import pallas as pl
from jax.experimental.pallas import tpu as pltpu
from jax.sharding import PartitionSpec as P

STEPS = 8
NF = 32
NANG = 128
NMAT = 4
NGX, NGY, NAF = 16, 4, 2
BX, BY, BZ = 32, 16, 128
HX = BX // 2
SLOTS = 8
DT = 0.5
MESH = pl.DeviceIdType.MESH
HIGHEST = lax.Precision.HIGHEST
F32 = jnp.float32


def tables():
    omega = 0.25 + 1.5 * np.arange(NF) / NF
    t = (np.arange(STEPS) + 1.0) * DT
    phase = t[:, None] * omega[None, :]
    weights = np.concatenate([np.cos(phase), -np.sin(phase)], axis=1) / STEPS
    angle = np.arange(NANG)
    rho = 0.25 + 0.7 * (angle + 0.5) / NANG
    s_y = rho * np.cos(2.0 * np.pi * angle / NANG)
    s_z = rho * np.sin(2.0 * np.pi * angle / NANG)
    z_phase = omega[:, None, None] * s_z[None, None, :] * np.arange(BZ)[None, :, None]
    z_table = np.concatenate([np.cos(z_phase), np.sin(z_phase)], axis=2)
    z_table = z_table.reshape(NGX, 2, BZ, 2 * NANG)
    y = np.arange(NGY * BY).reshape(NGY, 1, BY)
    z0 = (BZ * np.arange(NAF)).reshape(1, NAF, 1)
    shift = s_y * y[..., None] + s_z * z0[..., None]
    y_phase = omega[:, None, None] * shift[:, :, None]
    y_table = np.stack([np.cos(y_phase), np.sin(y_phase)], axis=3)
    y_table = y_table / math.sqrt(NGY * BY * NAF * BZ)
    y_table = y_table.reshape(NGY * NAF, NGX, 2, 2, BY, NANG)
    spread = np.broadcast_to(weights[:, :, None], (STEPS, 2 * NF, 128))
    return (
        weights.astype(np.float32),
        spread.astype(np.float32),
        z_table.astype(np.float32),
        y_table.astype(np.float32),
    )


def kernel(
    eps_ref, strength_ref, freq_ref, damp_ref, weight_ref, owner_ref,
    fields_ref, pol_ref, mat_ref, spread_hbm, ztab_hbm, ytab_hbm,
    out_f, out_p, out_s, out_far,
    E, H, PQ, mat, coef, stage, samp, ztab, ytab, spread, part, parts,
    local_sem, swap_send, swap_recv, halo_send, halo_recv, first_send, first_recv,
    samp_send, samp_recv, far_send, far_recv, out_sem, out_send, out_recv,
):
    gx, gy, c = lax.axis_index("gx"), lax.axis_index("gy"), lax.axis_index("af")
    place = 2 * gx + c
    other = 1 - c
    has_up, has_down = place < 2 * NGX - 1, place > 0
    has_right, has_left = gy < NGY - 1, gy > 0
    up = (gx + c, gy, other)
    down = (gx - other, gy, other)
    right, left = (gx, gy + 1, c), (gx, gy - 1, c)
    up_left = (gx + c, gy - 1, other)
    down_right = (gx - other, gy + 1, other)
    partner = (gx, gy, other)
    is_holder = jnp.logical_and(gx == NGX - 1, c == 1)
    me = gy * NAF + c

    barrier = pltpu.get_barrier_semaphore()

    def greet(device):
        pl.semaphore_signal(barrier, inc=1, device_id=device, device_id_type=MESH)

    for k in range(1, NGY * NAF):
        them = lax.rem(me + k, NGY * NAF)
        greet((gx, them // NAF, lax.rem(them, NAF)))
    across_up = jnp.logical_and(c == 1, has_up)
    across_down = jnp.logical_and(c == 0, has_down)
    across_up_left = jnp.logical_and(across_up, has_left)
    across_down_right = jnp.logical_and(across_down, has_right)
    for there, device in (
        (across_up, up), (across_down, down), (across_up_left, up_left), (across_down_right, down_right),
    ):
        @pl.when(there)
        def _(device=device):
            greet(device)

    @pl.when(jnp.logical_not(is_holder))
    def _():
        greet((NGX - 1, gy, 1))

    here = pl.ds(c * HX, HX)
    there = pl.ds(other * HX, HX)
    loads = [
        (fields_ref.at[0:3, here], E.at[0, :, c, 1:HX + 1, 8:24]),
        (fields_ref.at[3:6, here], H.at[:, c, 1:HX + 1, 8:24]),
        (pol_ref.at[:, :, here], PQ.at[:, :, c]),
        (mat_ref.at[here], mat.at[c]),
        (ztab_hbm.at[gx], ztab),
        (ytab_hbm.at[me, gx], ytab),
        (spread_hbm, spread),
    ]
    loads = [pltpu.make_async_copy(s, d, local_sem.at[i]) for i, (s, d) in enumerate(loads)]
    for copy in loads:
        copy.start()

    @pl.when(jnp.logical_not(has_up))
    def _():
        for p in range(2):
            for d in (1, 2):
                for z in range(2):
                    E[p, d, z, HX + 1, 0:24] = jnp.zeros((24, 128), F32)

    @pl.when(jnp.logical_not(has_right))
    def _():
        @pl.loop(0, HX + 1)
        def _(i):
            for p in range(2):
                for d in (0, 2):
                    for z in range(2):
                        E[p, d, z, i, 24:32] = jnp.zeros((8, 128), F32)

    count = (
        NGY * NAF - 1
        + across_up.astype(jnp.int32) + across_down.astype(jnp.int32)
        + across_up_left.astype(jnp.int32) + across_down_right.astype(jnp.int32)
        + jnp.where(is_holder, 2 * NGX - 1, 0)
    )
    pl.semaphore_wait(barrier, count)

    swaps = [
        (fields_ref.at[0:3, there], E.at[0, :, c, 1:HX + 1, 8:24]),
        (fields_ref.at[3:6, there], H.at[:, c, 1:HX + 1, 8:24]),
        (pol_ref.at[:, :, there], PQ.at[:, :, c]),
        (mat_ref.at[there], mat.at[c]),
    ]
    swaps = [
        pltpu.make_async_remote_copy(
            src_ref=s, dst_ref=d, send_sem=swap_send.at[i], recv_sem=swap_recv.at[i],
            device_id=partner, device_id_type=MESH,
        )
        for i, (s, d) in enumerate(swaps)
    ]
    for copy in swaps:
        copy.start()
    for i in range(2):
        loads[i].wait()
        swaps[i].wait()

    def halos(p):
        def message(k, src, dst, device):
            return pltpu.make_async_remote_copy(
                src_ref=src, dst_ref=dst, send_sem=halo_send.at[k], recv_sem=halo_recv.at[p, k],
                device_id=device, device_id_type=MESH,
            )

        own, rows = pl.ds(1, HX), pl.ds(8, BY)
        return [
            (has_up, has_down, message(0, E.at[p, :, :, HX, rows], E.at[p, :, :, 0, rows], up)),
            (has_down, has_up, message(1, E.at[p, 1:3, :, 1, rows], E.at[p, 1:3, :, HX + 1, rows], down)),
            (has_right, has_left, message(2, E.at[p, :, :, own, 23:24], E.at[p, :, :, own, 7:8], right)),
            (has_left, has_right, message(3, E.at[p, 0, :, own, 8:9], E.at[p, 0, :, own, 24:25], left)),
            (has_left, has_right, message(4, E.at[p, 2, :, own, 8:9], E.at[p, 2, :, own, 24:25], left)),
            (
                jnp.logical_and(has_up, has_left), jnp.logical_and(has_down, has_right),
                message(5, E.at[p, 0, :, HX, 8:9], E.at[p, 0, :, 0, 24:25], up_left),
            ),
            (
                jnp.logical_and(has_down, has_right), jnp.logical_and(has_up, has_left),
                message(6, E.at[p, 1, :, 1, 23:24], E.at[p, 1, :, HX + 1, 7:8], down_right),
            ),
        ]

    def start(messages):
        for receiver, _, copy in messages:
            @pl.when(receiver)
            def _(copy=copy):
                copy.start()

    def finish(messages):
        for receiver, sender, copy in messages:
            @pl.when(sender)
            def _(copy=copy):
                copy.wait_recv()

            @pl.when(receiver)
            def _(copy=copy):
                copy.wait_send()

    def first(k, src, dst, device):
        return pltpu.make_async_remote_copy(
            src_ref=src, dst_ref=dst, send_sem=first_send.at[k], recv_sem=first_recv.at[k],
            device_id=device, device_id_type=MESH,
        )

    own, rows = pl.ds(1, HX), pl.ds(8, BY)
    h_layers = [
        (has_up, has_down, first(0, H.at[1:3, :, HX, rows], H.at[1:3, :, 0, rows], up)),
        (has_right, has_left, first(1, H.at[0, :, own, 23:24], H.at[0, :, own, 7:8], right)),
        (has_right, has_left, first(2, H.at[2, :, own, 23:24], H.at[2, :, own, 7:8], right)),
    ]
    start(h_layers)
    start(halos(0))
    for i in range(2, 4):
        loads[i].wait()
        swaps[i].wait()
    for copy in loads[4:]:
        copy.wait()

    rates = [[], [], [], []]
    for m in range(NMAT):
        turning = jnp.full((8, 128), freq_ref[m], F32) * DT
        half_loss = jnp.full((8, 128), damp_ref[m], F32) * (0.5 * DT)
        denominator = 1.0 + half_loss
        rates[0].append((2.0 - turning * turning) / denominator)
        rates[1].append(-(1.0 - half_loss) / denominator)
        rates[2].append(jnp.full((8, 128), strength_ref[m], F32) * turning * turning / denominator)
        rates[3].append(1.0 / jnp.full((8, 128), eps_ref[m], F32))

    @pl.loop(0, HX)
    def _(i):
        for z in range(2):
            for j in range(2):
                cell = mat[z, i, 8 * j:8 * j + 8]
                for k in range(4):
                    value = jnp.where(cell == 1, rates[k][1], rates[k][0])
                    value = jnp.where(cell == 2, rates[k][2], value)
                    coef[k, z, i, 8 * j:8 * j + 8] = jnp.where(cell == 3, rates[k][3], value)

    finish(h_layers)

    lane = lax.broadcasted_iota(jnp.int32, (8, 128), 1)
    last_lane, first_lane = lane == 127, lane == 0

    def ahead_z(v):
        r0, r1 = (pltpu.roll(x, 127, 1) for x in v)
        return jnp.where(last_lane, r1, r0), jnp.where(last_lane, 0.0, r1)

    def behind_z(v):
        r0, r1 = (pltpu.roll(x, 1, 1) for x in v)
        return jnp.where(first_lane, 0.0, r0), jnp.where(first_lane, r0, r1)

    def magnetic(p, i, j, keep):
        r = pl.ds(8 * j, 8)
        r1 = pl.ds(8 * j + 1, 8)
        ex, ey, ez = ([E[p, d, z, i, r] for z in range(2)] for d in range(3))
        ex_z, ey_z = ahead_z(ex), ahead_z(ey)
        for z in range(2):
            hx = H[0, z, i, r] - DT * ((E[p, 2, z, i, r1] - ez[z]) - (ey_z[z] - ey[z]))
            hy = H[1, z, i, r] - DT * ((ex_z[z] - ex[z]) - (E[p, 2, z, i + 1, r] - ez[z]))
            hz = H[2, z, i, r] - DT * ((E[p, 1, z, i + 1, r] - ey[z]) - (E[p, 0, z, i, r1] - ex[z]))
            if keep is not None:
                hx, hy, hz = (jnp.where(keep, h, 0.0) for h in (hx, hy, hz))
            H[0, z, i, r] = hx
            H[1, z, i, r] = hy
            H[2, z, i, r] = hz

    def electric(p, i, j):
        q = 1 - p
        r = pl.ds(8 * j, 8)
        r1 = pl.ds(8 * j - 1, 8)
        s = pl.ds(8 * (j - 1), 8)
        hx, hy, hz = ([H[d, z, i, r] for z in range(2)] for d in range(3))
        hx_z, hy_z = behind_z(hx), behind_z(hy)
        for z in range(2):
            curl = (
                (hz[z] - H[2, z, i, r1]) - (hy[z] - hy_z[z]),
                (hx[z] - hx_z[z]) - (hz[z] - H[2, z, i - 1, r]),
                (hy[z] - H[1, z, i - 1, r]) - (hx[z] - H[0, z, i, r1]),
            )
            keep, back, drive, inverse = (coef[k, z, i - 1, s] for k in range(4))
            for d in range(3):
                e = E[p, d, z, i, r]
                now = PQ[p, d, z, i - 1, s]
                new = keep * now + back * PQ[q, d, z, i - 1, s] + drive * e
                PQ[q, d, z, i - 1, s] = new
                E[q, d, z, i, r] = e + inverse * (DT * curl[d] - (new - now))

    def sample_copy(n, g, t):
        return pltpu.make_async_remote_copy(
            src_ref=stage.at[n, t], dst_ref=samp.at[n], send_sem=samp_send.at[g, t], recv_sem=samp_recv.at[n],
            device_id=(g, gy, t), device_id_type=MESH,
        )

    def each_receiver(act):
        @pl.loop(0, NGX)
        def _(g):
            act(g, 0)

            @pl.when(g < NGX - 1)
            def _():
                act(g, 1)

    @pl.loop(0, STEPS)
    def _(n):
        p = lax.rem(n, 2)

        @pl.when(n > 0)
        def _():
            start(halos(p))

        finish(halos(p))
        magnetic(p, 0, 1, has_down)
        magnetic(p, 0, 2, has_down)

        @pl.loop(1, HX + 1)
        def _(i):
            magnetic(p, i, 0, has_left)
            magnetic(p, i, 1, None)
            magnetic(p, i, 2, None)

        @pl.loop(1, HX + 1)
        def _(i):
            electric(p, i, 1)
            electric(p, i, 2)

        @pl.when(is_holder)
        def _():
            @pl.when(n > 0)
            def _():
                each_receiver(lambda g, t: sample_copy(n - 1, g, t).wait_send())

            for t in range(2):
                for d in range(2):
                    stage[n, t, d] = E[1 - p, d + 1, t, 1, 8:24]
                    stage[n, t, d + 2] = H[d + 1, t, 1, 8:24]
            each_receiver(lambda g, t: sample_copy(n, g, t).start())
            samp[n] = stage[n, 1]

    e_out = lambda z: (E.at[0, :, z, own, rows], out_f.at[0:3, here])
    h_out = lambda z: (H.at[:, z, own, rows], out_f.at[3:6, here])
    p_out = lambda z: (PQ.at[:, :, z], out_p.at[:, :, here])
    sends = []
    for k, out in enumerate((e_out, h_out, p_out)):
        s, d = out(other)
        sends.append(pltpu.make_async_remote_copy(
            src_ref=s, dst_ref=d, send_sem=out_send.at[k], recv_sem=out_recv.at[k],
            device_id=partner, device_id_type=MESH,
        ))
        s, d = out(c)
        sends.append(pltpu.make_async_copy(s, d, out_sem.at[k]))
    for copy in sends:
        copy.start()

    @pl.when(is_holder)
    def _():
        each_receiver(lambda g, t: sample_copy(STEPS - 1, g, t).wait_send())

    @pl.when(jnp.logical_not(is_holder))
    def _():
        for n in range(STEPS):
            sample_copy(n, 0, 0).wait_recv()

    rows_of = [samp[n].reshape(4 * BY, 128) for n in range(STEPS)]
    for f in range(2):
        real = weight_ref[0, 2 * gx + f] * rows_of[0]
        imag = weight_ref[0, NF + 2 * gx + f] * rows_of[0]
        for n in range(1, STEPS):
            real += weight_ref[n, 2 * gx + f] * rows_of[n]
            imag += weight_ref[n, NF + 2 * gx + f] * rows_of[n]
        both = jnp.concatenate([real, imag], axis=0)
        inner = jnp.dot(both, ztab[f], precision=HIGHEST, preferred_element_type=F32)
        inner_real = inner[:64, :128] - inner[64:, 128:]
        inner_imag = inner[:64, 128:] + inner[64:, :128]
        cos_y, sin_y = ytab[f, 0], ytab[f, 1]
        lines = []
        for d in range(4):
            re, im = inner_real[16 * d:16 * d + 16], inner_imag[16 * d:16 * d + 16]
            lines.append(jnp.sum(re * cos_y - im * sin_y, axis=0, keepdims=True))
            lines.append(jnp.sum(re * sin_y + im * cos_y, axis=0, keepdims=True))
        part[f] = jnp.concatenate(lines, axis=0)

    far = []
    for k in range(1, NGY * NAF):
        them = lax.rem(me + k, NGY * NAF)
        far.append(pltpu.make_async_remote_copy(
            src_ref=part.at[them // 4], dst_ref=parts.at[k], send_sem=far_send.at[k], recv_sem=far_recv.at[k],
            device_id=(gx, them // NAF, lax.rem(them, NAF)), device_id_type=MESH,
        ))
    for copy in far:
        copy.start()

    mine = (owner_ref[...] == gx).astype(F32)
    row = lax.broadcasted_iota(jnp.int32, (64, 64), 0)
    col = lax.broadcasted_iota(jnp.int32, (64, 64), 1)
    rank = jnp.dot((col < row).astype(F32), mine, precision=HIGHEST, preferred_element_type=F32)
    slot = lax.broadcasted_iota(jnp.int32, (64, 128), 1).astype(F32)
    picked = jnp.where(rank == slot, mine, 0.0)
    chosen = [
        lax.dot_general(picked, rows_of[n], (((0,), (0,)), ((), ())), precision=HIGHEST, preferred_element_type=F32)
        for n in range(STEPS)
    ]
    for s in range(SLOTS):
        for k in range(2 * NF // 8):
            total = spread[0, 8 * k:8 * k + 8] * chosen[0][s:s + 1]
            for n in range(1, STEPS):
                total += spread[n, 8 * k:8 * k + 8] * chosen[n][s:s + 1]
            out_s[0, 0, 0, s, 8 * k:8 * k + 8] = total

    total = part[me // 4]
    for k in range(1, NGY * NAF):
        far[k - 1].wait()
        total += parts[k]
    block = lax.rem(me, 4)
    total = pltpu.roll(total, lax.rem(128 - 32 * block, 128), 1)
    out_far[...] = total[:, :32]
    for copy in sends:
        copy.wait()


def on_device(constants, fields, polarization, material, eps_inf, pole_strength, pole_freq, damping, owner):
    weights, spread, z_table, y_table = constants
    smem = pl.BlockSpec(memory_space=pltpu.SMEM)
    vmem = pl.BlockSpec(memory_space=pltpu.VMEM)
    hbm = pl.BlockSpec(memory_space=pl.ANY)
    dma = lambda *shape: pltpu.SemaphoreType.DMA(shape)
    return pl.pallas_call(
        kernel,
        out_shape=(
            jax.ShapeDtypeStruct(fields.shape, F32),
            jax.ShapeDtypeStruct(polarization.shape, F32),
            jax.ShapeDtypeStruct((1, 1, 1, SLOTS, 2 * NF, BZ), F32),
            jax.ShapeDtypeStruct((8, 32), F32),
        ),
        in_specs=[smem] * 5 + [vmem] + [hbm] * 6,
        out_specs=(hbm, hbm, vmem, vmem),
        scratch_shapes=[
            pltpu.VMEM((2, 3, 2, HX + 2, 32, 128), F32),
            pltpu.VMEM((3, 2, HX + 1, 24, 128), F32),
            pltpu.VMEM((2, 3, 2, HX, BY, 128), F32),
            pltpu.VMEM((2, HX, BY, 128), jnp.int32),
            pltpu.VMEM((4, 2, HX, BY, 128), F32),
            pltpu.VMEM((STEPS, 2, 4, BY, 128), F32),
            pltpu.VMEM((STEPS, 4, BY, 128), F32),
            pltpu.VMEM((2, BZ, 2 * NANG), F32),
            pltpu.VMEM((2, 2, BY, NANG), F32),
            pltpu.VMEM((STEPS, 2 * NF, 128), F32),
            pltpu.VMEM((2, 8, 128), F32),
            pltpu.VMEM((8, 8, 128), F32),
            dma(7), dma(4), dma(4), dma(7), dma(2, 7), dma(3), dma(3),
            dma(NGX, 2), dma(STEPS), dma(8), dma(8), dma(3), dma(3), dma(3),
        ],
        compiler_params=pltpu.CompilerParams(
            collective_id=0, has_side_effects=True, vmem_limit_bytes=56 << 20
        ),
        name="fdtd",
    )(
        eps_inf, pole_strength, pole_freq, damping, weights, owner.reshape(64, 1),
        fields, polarization, material, spread, z_table, y_table,
    )


def solution(mesh):
    constants = tables()

    def whole(*arguments):
        return on_device(tuple(jnp.asarray(x) for x in constants), *arguments)

    return jax.shard_map(
        whole,
        mesh=mesh,
        in_specs=(
            P(None, "gx", "gy", "af"),
            P(None, None, "gx", "gy", "af"),
            P("gx", "gy", "af"),
            P(), P(), P(), P(),
            P("gy", "af", None, None),
        ),
        out_specs=(
            P(None, "gx", "gy", "af"),
            P(None, None, "gx", "gy", "af"),
            P("gx", "gy", "af", None, None, None),
            P(None, ("gx", "gy", "af")),
        ),
        check_vma=False,
    )
```

```python
import functools
import math

import jax
import jax.numpy as jnp
import numpy as np
from jax import lax
from jax.experimental import pallas as pl
from jax.experimental.pallas import tpu as pltpu
from jax.sharding import PartitionSpec as P

STEPS = 8
NF = 32
NANG = 128
NMAT = 4
NGX, NGY, NAF = 16, 4, 2
BX, BY, BZ = 32, 16, 128
HX = BX // 2
SLOTS = 8
DT = 0.5
MESH = pl.DeviceIdType.MESH
HIGHEST = lax.Precision.HIGHEST
F32 = jnp.float32


def tables():
    omega = 0.25 + 1.5 * np.arange(NF) / NF
    t = (np.arange(STEPS) + 1.0) * DT
    phase = t[:, None] * omega[None, :]
    weights = np.concatenate([np.cos(phase), -np.sin(phase)], axis=1) / STEPS
    angle = np.arange(NANG)
    rho = 0.25 + 0.7 * (angle + 0.5) / NANG
    s_y = rho * np.cos(2.0 * np.pi * angle / NANG)
    s_z = rho * np.sin(2.0 * np.pi * angle / NANG)
    z_phase = omega[:, None, None] * s_z[None, None, :] * np.arange(BZ)[None, :, None]
    z_table = np.concatenate([np.cos(z_phase), np.sin(z_phase)], axis=2)
    z_table = z_table.reshape(NGX, 2, BZ, 2 * NANG)
    y = np.arange(NGY * BY).reshape(NGY, 1, BY)
    z0 = (BZ * np.arange(NAF)).reshape(1, NAF, 1)
    shift = s_y * y[..., None] + s_z * z0[..., None]
    y_phase = omega[:, None, None] * shift[:, :, None]
    y_table = np.stack([np.cos(y_phase), np.sin(y_phase)], axis=3)
    y_table = y_table / math.sqrt(NGY * BY * NAF * BZ)
    y_table = y_table.reshape(NGY * NAF, NGX, 2, 2, BY, NANG)
    spread = np.broadcast_to(weights[:, :, None], (STEPS, 2 * NF, 128))
    return (
        weights.astype(np.float32),
        spread.astype(np.float32),
        z_table.astype(np.float32),
        y_table.astype(np.float32),
    )


def kernel(
    eps_ref, strength_ref, freq_ref, damp_ref, weight_ref, owner_ref,
    fields_ref, pol_ref, mat_ref, spread_hbm, ztab_hbm, ytab_hbm,
    out_f, out_p, out_s, out_far,
    E0, E1, H, P0, P1, mat, coef, stage, samp, ztab, ytab, spread, part, parts,
    local_sem, swap_send, swap_recv, halo_send, halo_recv, first_send, first_recv,
    samp_send, samp_recv, far_send, far_recv, out_sem, out_send, out_recv,
):
    gx, gy, c = lax.axis_index("gx"), lax.axis_index("gy"), lax.axis_index("af")
    place = 2 * gx + c
    E = (E0, E1)
    other = 1 - c
    has_up, has_down = place < 2 * NGX - 1, place > 0
    has_right, has_left = gy < NGY - 1, gy > 0
    up = (gx + c, gy, other)
    down = (gx - other, gy, other)
    right, left = (gx, gy + 1, c), (gx, gy - 1, c)
    up_left = (gx + c, gy - 1, other)
    down_right = (gx - other, gy + 1, other)
    partner = (gx, gy, other)
    is_holder = jnp.logical_and(gx == NGX - 1, c == 1)
    me = gy * NAF + c

    barrier = pltpu.get_barrier_semaphore()

    def greet(device):
        pl.semaphore_signal(barrier, inc=1, device_id=device, device_id_type=MESH)

    for k in range(1, NGY * NAF):
        them = lax.rem(me + k, NGY * NAF)
        greet((gx, them // NAF, lax.rem(them, NAF)))
    across_up = jnp.logical_and(c == 1, has_up)
    across_down = jnp.logical_and(c == 0, has_down)
    across_up_left = jnp.logical_and(across_up, has_left)
    across_down_right = jnp.logical_and(across_down, has_right)
    for there, device in (
        (across_up, up), (across_down, down), (across_up_left, up_left), (across_down_right, down_right),
    ):
        @pl.when(there)
        def _(device=device):
            greet(device)

    @pl.when(jnp.logical_not(is_holder))
    def _():
        greet((NGX - 1, gy, 1))

    here = pl.ds(c * HX, HX)
    there = pl.ds(other * HX, HX)
    loads = [
        (fields_ref.at[0:3, here], E0.at[:, c, 1:HX + 1, 8:24]),
        (fields_ref.at[3:6, here], H.at[:, c, 1:HX + 1, 8:24]),
        (pol_ref.at[0, :, here], P0.at[:, c]),
        (pol_ref.at[1, :, here], P1.at[:, c]),
        (mat_ref.at[here], mat.at[c]),
        (ztab_hbm.at[gx], ztab),
        (ytab_hbm.at[me, gx], ytab),
        (spread_hbm, spread),
    ]
    loads = [pltpu.make_async_copy(s, d, local_sem.at[i]) for i, (s, d) in enumerate(loads)]
    for copy in loads:
        copy.start()

    @pl.when(jnp.logical_not(has_up))
    def _():
        for p in range(2):
            for d in (1, 2):
                for z in range(2):
                    E[p][d, z, HX + 1, 0:24] = jnp.zeros((24, 128), F32)

    @pl.when(jnp.logical_not(has_right))
    def _():
        @pl.loop(0, HX + 1)
        def _(i):
            for p in range(2):
                for d in (0, 2):
                    for z in range(2):
                        E[p][d, z, i, 24:32] = jnp.zeros((8, 128), F32)

    count = (
        NGY * NAF - 1
        + across_up.astype(jnp.int32) + across_down.astype(jnp.int32)
        + across_up_left.astype(jnp.int32) + across_down_right.astype(jnp.int32)
        + jnp.where(is_holder, 2 * NGX - 1, 0)
    )
    pl.semaphore_wait(barrier, count)

    swaps = [
        (fields_ref.at[0:3, there], E0.at[:, c, 1:HX + 1, 8:24]),
        (fields_ref.at[3:6, there], H.at[:, c, 1:HX + 1, 8:24]),
        (pol_ref.at[0, :, there], P0.at[:, c]),
        (pol_ref.at[1, :, there], P1.at[:, c]),
        (mat_ref.at[there], mat.at[c]),
    ]
    swaps = [
        pltpu.make_async_remote_copy(
            src_ref=s, dst_ref=d, send_sem=swap_send.at[i], recv_sem=swap_recv.at[i],
            device_id=partner, device_id_type=MESH,
        )
        for i, (s, d) in enumerate(swaps)
    ]
    for copy in swaps:
        copy.start()
    for i in range(2):
        loads[i].wait()
        swaps[i].wait()

    def halos(p):
        def message(k, src, dst, device):
            return pltpu.make_async_remote_copy(
                src_ref=src, dst_ref=dst, send_sem=halo_send.at[k], recv_sem=halo_recv.at[p, k],
                device_id=device, device_id_type=MESH,
            )

        e = E[p]
        own, rows = pl.ds(1, HX), pl.ds(8, BY)
        return [
            (has_up, has_down, message(0, e.at[:, :, HX, rows], e.at[:, :, 0, rows], up)),
            (has_down, has_up, message(1, e.at[1:3, :, 1, rows], e.at[1:3, :, HX + 1, rows], down)),
            (has_right, has_left, message(2, e.at[:, :, own, 23:24], e.at[:, :, own, 7:8], right)),
            (has_left, has_right, message(3, e.at[0, :, own, 8:9], e.at[0, :, own, 24:25], left)),
            (has_left, has_right, message(4, e.at[2, :, own, 8:9], e.at[2, :, own, 24:25], left)),
            (
                jnp.logical_and(has_up, has_left), jnp.logical_and(has_down, has_right),
                message(5, e.at[0, :, HX, 8:9], e.at[0, :, 0, 24:25], up_left),
            ),
            (
                jnp.logical_and(has_down, has_right), jnp.logical_and(has_up, has_left),
                message(6, e.at[1, :, 1, 23:24], e.at[1, :, HX + 1, 7:8], down_right),
            ),
        ]

    def start(messages):
        for receiver, _, copy in messages:
            @pl.when(receiver)
            def _(copy=copy):
                copy.start()

    def finish(messages):
        for receiver, sender, copy in messages:
            @pl.when(sender)
            def _(copy=copy):
                copy.wait_recv()

            @pl.when(receiver)
            def _(copy=copy):
                copy.wait_send()

    def first(k, src, dst, device):
        return pltpu.make_async_remote_copy(
            src_ref=src, dst_ref=dst, send_sem=first_send.at[k], recv_sem=first_recv.at[k],
            device_id=device, device_id_type=MESH,
        )

    own, rows = pl.ds(1, HX), pl.ds(8, BY)
    h_layers = [
        (has_up, has_down, first(0, H.at[1:3, :, HX, rows], H.at[1:3, :, 0, rows], up)),
        (has_right, has_left, first(1, H.at[0, :, own, 23:24], H.at[0, :, own, 7:8], right)),
        (has_right, has_left, first(2, H.at[2, :, own, 23:24], H.at[2, :, own, 7:8], right)),
    ]
    start(h_layers)
    start(halos(0))
    for i in range(2, 5):
        loads[i].wait()
        swaps[i].wait()
    for copy in loads[5:]:
        copy.wait()

    rates = [[], [], [], []]
    for m in range(NMAT):
        turning = jnp.full((8, 128), freq_ref[m], F32) * DT
        half_loss = jnp.full((8, 128), damp_ref[m], F32) * (0.5 * DT)
        denominator = 1.0 + half_loss
        rates[0].append((2.0 - turning * turning) / denominator)
        rates[1].append(-(1.0 - half_loss) / denominator)
        rates[2].append(jnp.full((8, 128), strength_ref[m], F32) * turning * turning / denominator)
        rates[3].append(1.0 / jnp.full((8, 128), eps_ref[m], F32))

    @pl.loop(0, HX)
    def _(i):
        for z in range(2):
            for j in range(2):
                cell = mat[z, i, 8 * j:8 * j + 8]
                for k in range(4):
                    value = jnp.where(cell == 1, rates[k][1], rates[k][0])
                    value = jnp.where(cell == 2, rates[k][2], value)
                    coef[k, z, i, 8 * j:8 * j + 8] = jnp.where(cell == 3, rates[k][3], value)

    finish(h_layers)

    lane = lax.broadcasted_iota(jnp.int32, (8, 128), 1)
    last_lane, first_lane = lane == 127, lane == 0

    def ahead_z(v):
        r0, r1 = (pltpu.roll(x, 127, 1) for x in v)
        return jnp.where(last_lane, r1, r0), jnp.where(last_lane, 0.0, r1)

    def behind_z(v):
        r0, r1 = (pltpu.roll(x, 1, 1) for x in v)
        return jnp.where(first_lane, 0.0, r0), jnp.where(first_lane, r0, r1)

    def magnetic(e, i, j, keep=None):
        r = pl.ds(8 * j, 8)
        r1 = pl.ds(8 * j + 1, 8)
        ex, ey, ez = ([e[d, z, i, r] for z in range(2)] for d in range(3))
        ex_z, ey_z = ahead_z(ex), ahead_z(ey)
        for z in range(2):
            hx = H[0, z, i, r] - DT * ((e[2, z, i, r1] - ez[z]) - (ey_z[z] - ey[z]))
            hz = H[2, z, i, r] - DT * ((e[1, z, i + 1, r] - ey[z]) - (e[0, z, i, r1] - ex[z]))
            H[0, z, i, r] = hx if keep is None else jnp.where(keep, hx, 0.0)
            H[2, z, i, r] = hz if keep is None else jnp.where(keep, hz, 0.0)
            if j > 0:
                hy = H[1, z, i, r] - DT * ((ex_z[z] - ex[z]) - (e[2, z, i + 1, r] - ez[z]))
                H[1, z, i, r] = hy if keep is None else jnp.where(keep, hy, 0.0)

    def electric(e, e_new, now_ref, old_ref, i, j):
        r = pl.ds(8 * j, 8)
        r1 = pl.ds(8 * j - 1, 8)
        s = pl.ds(8 * (j - 1), 8)
        hx, hy, hz = ([H[d, z, i, r] for z in range(2)] for d in range(3))
        hx_z, hy_z = behind_z(hx), behind_z(hy)
        for z in range(2):
            curl = (
                (hz[z] - H[2, z, i, r1]) - (hy[z] - hy_z[z]),
                (hx[z] - hx_z[z]) - (hz[z] - H[2, z, i - 1, r]),
                (hy[z] - H[1, z, i - 1, r]) - (hx[z] - H[0, z, i, r1]),
            )
            keep, back, drive, inverse = (coef[k, z, i - 1, s] for k in range(4))
            for d in range(3):
                value = e[d, z, i, r]
                now = now_ref[d, z, i - 1, s]
                new = keep * now + back * old_ref[d, z, i - 1, s] + drive * value
                old_ref[d, z, i - 1, s] = new
                e_new[d, z, i, r] = value + inverse * (DT * curl[d] - (new - now))

    def sample_copy(n, g, t):
        return pltpu.make_async_remote_copy(
            src_ref=stage.at[n, t], dst_ref=samp.at[n], send_sem=samp_send.at[g, t], recv_sem=samp_recv.at[n],
            device_id=(g, gy, t), device_id_type=MESH,
        )

    def each_receiver(act):
        @pl.loop(0, NGX)
        def _(g):
            act(g, 0)

            @pl.when(g < NGX - 1)
            def _():
                act(g, 1)

    def start_next(n, p):
        @pl.when(n < STEPS - 1)
        def _():
            start(halos(p))

    def step(n, p):
        e, e_new = E[p], E[1 - p]
        now_ref, old_ref = (P0, P1) if p == 0 else (P1, P0)

        @pl.loop(0, 3)
        def _(b):
            for u in range(5):
                magnetic(e, 1 + 5 * b + u, 1)

        finish(halos(p))
        magnetic(e, 0, 1, has_down)
        magnetic(e, 0, 2, has_down)
        magnetic(e, HX, 1)

        @pl.loop(0, 2)
        def _(b):
            for u in range(8):
                magnetic(e, 1 + 8 * b + u, 0, has_left)
                magnetic(e, 1 + 8 * b + u, 2)

        @pl.loop(0, 4)
        def _(b):
            for u in range(4):
                electric(e, e_new, now_ref, old_ref, 1 + 4 * b + u, 1)
                electric(e, e_new, now_ref, old_ref, 1 + 4 * b + u, 2)

        start_next(n, 1 - p)

        @pl.when(is_holder)
        def _():
            @pl.when(n > 0)
            def _():
                each_receiver(lambda g, t: sample_copy(n - 1, g, t).wait_send())

            for t in range(2):
                for d in range(2):
                    stage[n, t, d] = e_new[d + 1, t, 1, 8:24]
                    stage[n, t, d + 2] = H[d + 1, t, 1, 8:24]
            each_receiver(lambda g, t: sample_copy(n, g, t).start())
            samp[n] = stage[n, 1]

    @pl.loop(0, STEPS // 2)
    def _(b):
        step(2 * b, 0)
        step(2 * b + 1, 1)

    e_out = lambda z: (E0.at[:, z, own, rows], out_f.at[0:3, here])
    h_out = lambda z: (H.at[:, z, own, rows], out_f.at[3:6, here])
    p_out = lambda z: (P0.at[:, z], out_p.at[0, :, here])
    q_out = lambda z: (P1.at[:, z], out_p.at[1, :, here])
    sends = []
    for k, out in enumerate((e_out, h_out, p_out, q_out)):
        s, d = out(other)
        sends.append(pltpu.make_async_remote_copy(
            src_ref=s, dst_ref=d, send_sem=out_send.at[k], recv_sem=out_recv.at[k],
            device_id=partner, device_id_type=MESH,
        ))
        s, d = out(c)
        sends.append(pltpu.make_async_copy(s, d, out_sem.at[k]))
    for copy in sends:
        copy.start()

    @pl.when(is_holder)
    def _():
        each_receiver(lambda g, t: sample_copy(STEPS - 1, g, t).wait_send())

    @pl.when(jnp.logical_not(is_holder))
    def _():
        for n in range(STEPS):
            sample_copy(n, 0, 0).wait_recv()

    rows_of = [samp[n].reshape(4 * BY, 128) for n in range(STEPS)]
    for f in range(2):
        real = weight_ref[0, 2 * gx + f] * rows_of[0]
        imag = weight_ref[0, NF + 2 * gx + f] * rows_of[0]
        for n in range(1, STEPS):
            real += weight_ref[n, 2 * gx + f] * rows_of[n]
            imag += weight_ref[n, NF + 2 * gx + f] * rows_of[n]
        both = jnp.concatenate([real, imag], axis=0)
        inner = jnp.dot(both, ztab[f], precision=HIGHEST, preferred_element_type=F32)
        inner_real = inner[:64, :128] - inner[64:, 128:]
        inner_imag = inner[:64, 128:] + inner[64:, :128]
        cos_y, sin_y = ytab[f, 0], ytab[f, 1]
        lines = []
        for d in range(4):
            re, im = inner_real[16 * d:16 * d + 16], inner_imag[16 * d:16 * d + 16]
            lines.append(jnp.sum(re * cos_y - im * sin_y, axis=0, keepdims=True))
            lines.append(jnp.sum(re * sin_y + im * cos_y, axis=0, keepdims=True))
        part[f] = jnp.concatenate(lines, axis=0)

    far = []
    for k in range(1, NGY * NAF):
        them = lax.rem(me + k, NGY * NAF)
        far.append(pltpu.make_async_remote_copy(
            src_ref=part.at[them // 4], dst_ref=parts.at[k], send_sem=far_send.at[k], recv_sem=far_recv.at[k],
            device_id=(gx, them // NAF, lax.rem(them, NAF)), device_id_type=MESH,
        ))
    for copy in far:
        copy.start()

    mine = (owner_ref[...] == gx).astype(F32)
    row = lax.broadcasted_iota(jnp.int32, (64, 64), 0)
    col = lax.broadcasted_iota(jnp.int32, (64, 64), 1)
    rank = jnp.dot(
        jnp.broadcast_to(mine, (8, 64)), (row < col).astype(F32), precision=HIGHEST, preferred_element_type=F32
    )
    slot = lax.broadcasted_iota(jnp.int32, (8, 64), 0).astype(F32)
    picked = jnp.where(rank == slot, mine, 0.0)
    chosen = [
        jnp.dot(picked, rows_of[n], precision=HIGHEST, preferred_element_type=F32) for n in range(STEPS)
    ]
    for s in range(SLOTS):
        for k in range(2 * NF // 8):
            total = spread[0, 8 * k:8 * k + 8] * chosen[0][s:s + 1]
            for n in range(1, STEPS):
                total += spread[n, 8 * k:8 * k + 8] * chosen[n][s:s + 1]
            out_s[0, 0, 0, s, 8 * k:8 * k + 8] = total

    total = part[me // 4]
    for k in range(1, NGY * NAF):
        far[k - 1].wait()
        total += parts[k]
    block = lax.rem(me, 4)
    total = pltpu.roll(total, lax.rem(128 - 32 * block, 128), 1)
    out_far[...] = total[:, :32]
    for copy in sends:
        copy.wait()


def on_device(constants, fields, polarization, material, eps_inf, pole_strength, pole_freq, damping, owner):
    weights, spread, z_table, y_table = constants
    smem = pl.BlockSpec(memory_space=pltpu.SMEM)
    vmem = pl.BlockSpec(memory_space=pltpu.VMEM)
    hbm = pl.BlockSpec(memory_space=pl.ANY)
    dma = lambda *shape: pltpu.SemaphoreType.DMA(shape)
    return pl.pallas_call(
        kernel,
        out_shape=(
            pltpu.VMEM(fields.shape, F32),
            pltpu.VMEM(polarization.shape, F32),
            pltpu.VMEM((1, 1, 1, SLOTS, 2 * NF, BZ), F32),
            pltpu.VMEM((8, 32), F32),
        ),
        in_specs=[smem] * 5 + [vmem] + [hbm] * 6,
        out_specs=(vmem, vmem, vmem, vmem),
        scratch_shapes=[
            pltpu.VMEM((3, 2, HX + 2, 32, 128), F32),
            pltpu.VMEM((3, 2, HX + 2, 32, 128), F32),
            pltpu.VMEM((3, 2, HX + 1, 24, 128), F32),
            pltpu.VMEM((3, 2, HX, BY, 128), F32),
            pltpu.VMEM((3, 2, HX, BY, 128), F32),
            pltpu.VMEM((2, HX, BY, 128), jnp.int32),
            pltpu.VMEM((4, 2, HX, BY, 128), F32),
            pltpu.VMEM((STEPS, 2, 4, BY, 128), F32),
            pltpu.VMEM((STEPS, 4, BY, 128), F32),
            pltpu.VMEM((2, BZ, 2 * NANG), F32),
            pltpu.VMEM((2, 2, BY, NANG), F32),
            pltpu.VMEM((STEPS, 2 * NF, 128), F32),
            pltpu.VMEM((2, 8, 128), F32),
            pltpu.VMEM((8, 8, 128), F32),
            dma(8), dma(5), dma(5), dma(7), dma(2, 7), dma(3), dma(3),
            dma(NGX, 2), dma(STEPS), dma(8), dma(8), dma(4), dma(4), dma(4),
        ],
        compiler_params=pltpu.CompilerParams(
            collective_id=0, has_side_effects=True, vmem_limit_bytes=56 << 20
        ),
        name="fdtd",
    )(
        eps_inf, pole_strength, pole_freq, damping, weights, owner.reshape(1, 64),
        fields, polarization, material, spread, z_table, y_table,
    )


def solution(mesh):
    constants = tables()

    def whole(*arguments):
        return on_device(tuple(jnp.asarray(x) for x in constants), *arguments)

    return jax.shard_map(
        whole,
        mesh=mesh,
        in_specs=(
            P(None, "gx", "gy", "af"),
            P(None, None, "gx", "gy", "af"),
            P("gx", "gy", "af"),
            P(), P(), P(), P(),
            P("gy", "af", None, None),
        ),
        out_specs=(
            P(None, "gx", "gy", "af"),
            P(None, None, "gx", "gy", "af"),
            P("gx", "gy", "af", None, None, None),
            P(None, ("gx", "gy", "af")),
        ),
        check_vma=False,
    )
```

```python
import functools
import math

import jax
import jax.numpy as jnp
import numpy as np
from jax import lax
from jax.experimental import pallas as pl
from jax.experimental.pallas import tpu as pltpu
from jax.sharding import PartitionSpec as P

STEPS = 8
NF = 32
NANG = 128
NMAT = 4
NGX, NGY, NAF = 16, 4, 2
BX, BY, BZ = 32, 16, 128
HX = BX // 2
ROW = 4
SLOTS = 8
DT = 0.5
MESH = pl.DeviceIdType.MESH
HIGHEST = lax.Precision.HIGHEST
F32 = jnp.float32


def tables():
    omega = 0.25 + 1.5 * np.arange(NF) / NF
    t = (np.arange(STEPS) + 1.0) * DT
    phase = t[:, None] * omega[None, :]
    weights = np.concatenate([np.cos(phase), -np.sin(phase)], axis=1) / STEPS
    angle = np.arange(NANG)
    rho = 0.25 + 0.7 * (angle + 0.5) / NANG
    s_y = rho * np.cos(2.0 * np.pi * angle / NANG)
    s_z = rho * np.sin(2.0 * np.pi * angle / NANG)
    z_phase = omega[:, None, None] * s_z[None, None, :] * np.arange(BZ)[None, :, None]
    z_table = np.concatenate([np.cos(z_phase), np.sin(z_phase)], axis=2)
    z_table = z_table.reshape(NGX, 2, BZ, 2 * NANG)
    y = np.arange(NGY * BY).reshape(NGY, 1, BY)
    z0 = (BZ * np.arange(NAF)).reshape(1, NAF, 1)
    shift = s_y * y[..., None] + s_z * z0[..., None]
    y_phase = omega[:, None, None] * shift[:, :, None]
    y_table = np.stack([np.cos(y_phase), np.sin(y_phase)], axis=3)
    y_table = y_table / math.sqrt(NGY * BY * NAF * BZ)
    y_table = y_table.reshape(NGY * NAF, NGX, 2, 2, BY, NANG)
    spread = np.broadcast_to(weights[:, :, None], (STEPS, 2 * NF, 128))
    return (
        weights.astype(np.float32),
        spread.astype(np.float32),
        z_table.astype(np.float32),
        y_table.astype(np.float32),
    )


def kernel(
    eps_ref, strength_ref, freq_ref, damp_ref, weight_ref, owner_ref,
    fields_ref, pol_ref, mat_ref, spread_hbm, ztab_hbm, ytab_hbm,
    out_f, out_p, out_s, out_far,
    E0, E1, H, P0, P1, mat, coef, stage, samp, ztab, ytab, spread, part, parts,
    local_sem, swap_send, swap_recv, halo_send, halo_recv, first_send, first_recv,
    samp_send, samp_recv, far_send, far_recv, out_sem, out_send, out_recv,
):
    gx, gy, c = lax.axis_index("gx"), lax.axis_index("gy"), lax.axis_index("af")
    place = 2 * gx + c
    E = (E0, E1)
    other = 1 - c
    has_up, has_down = place < 2 * NGX - 1, place > 0
    has_right, has_left = gy < NGY - 1, gy > 0
    up = (gx + c, gy, other)
    down = (gx - other, gy, other)
    right, left = (gx, gy + 1, c), (gx, gy - 1, c)
    up_left = (gx + c, gy - 1, other)
    down_right = (gx - other, gy + 1, other)
    partner = (gx, gy, other)
    is_holder = jnp.logical_and(gx == NGX - 1, c == 1)
    row_end = gx // ROW * ROW + ROW - 1
    is_last_row = gx // ROW == NGX // ROW - 1
    is_relay = jnp.logical_and(gx == row_end, jnp.logical_not(is_last_row))
    fed_by_relay = jnp.logical_and(gx != row_end, jnp.logical_not(is_last_row))
    fed_by_holder = jnp.logical_or(is_relay, jnp.logical_and(is_last_row, gx != row_end))
    me = gy * NAF + c

    barrier = pltpu.get_barrier_semaphore()

    def greet(device):
        pl.semaphore_signal(barrier, inc=1, device_id=device, device_id_type=MESH)

    for k in range(1, NGY * NAF):
        them = lax.rem(me + k, NGY * NAF)
        greet((gx, them // NAF, lax.rem(them, NAF)))
    across_up = jnp.logical_and(c == 1, has_up)
    across_down = jnp.logical_and(c == 0, has_down)
    across_up_left = jnp.logical_and(across_up, has_left)
    across_down_right = jnp.logical_and(across_down, has_right)
    for there, device in (
        (across_up, up), (across_down, down), (across_up_left, up_left), (across_down_right, down_right),
    ):
        @pl.when(there)
        def _(device=device):
            greet(device)

    @pl.when(fed_by_relay)
    def _():
        greet((row_end, gy, c))

    @pl.when(fed_by_holder)
    def _():
        greet((NGX - 1, gy, 1))

    here = pl.ds(c * HX, HX)
    there = pl.ds(other * HX, HX)
    loads = [
        (fields_ref.at[0:3, here], E0.at[:, c, 1:HX + 1, 8:24]),
        (fields_ref.at[3:6, here], H.at[:, c, 1:HX + 1, 8:24]),
        (pol_ref.at[0, :, here], P0.at[:, c]),
        (pol_ref.at[1, :, here], P1.at[:, c]),
        (mat_ref.at[here], mat.at[c]),
        (ztab_hbm.at[gx], ztab),
        (ytab_hbm.at[me, gx], ytab),
        (spread_hbm, spread),
    ]
    loads = [pltpu.make_async_copy(s, d, local_sem.at[i]) for i, (s, d) in enumerate(loads)]
    for copy in loads:
        copy.start()

    @pl.when(jnp.logical_not(has_up))
    def _():
        for p in range(2):
            for d in (1, 2):
                for z in range(2):
                    E[p][d, z, HX + 1, 0:24] = jnp.zeros((24, 128), F32)

    @pl.when(jnp.logical_not(has_right))
    def _():
        @pl.loop(0, HX + 1)
        def _(i):
            for p in range(2):
                for d in (0, 2):
                    for z in range(2):
                        E[p][d, z, i, 24:32] = jnp.zeros((8, 128), F32)

    count = (
        NGY * NAF - 1
        + across_up.astype(jnp.int32) + across_down.astype(jnp.int32)
        + across_up_left.astype(jnp.int32) + across_down_right.astype(jnp.int32)
        + jnp.where(is_holder, 2 * (NGX // ROW + ROW - 2), 0)
        + jnp.where(is_relay, ROW - 1, 0)
    )
    pl.semaphore_wait(barrier, count)

    swaps = [
        (fields_ref.at[0:3, there], E0.at[:, c, 1:HX + 1, 8:24]),
        (fields_ref.at[3:6, there], H.at[:, c, 1:HX + 1, 8:24]),
        (pol_ref.at[0, :, there], P0.at[:, c]),
        (pol_ref.at[1, :, there], P1.at[:, c]),
        (mat_ref.at[there], mat.at[c]),
    ]
    swaps = [
        pltpu.make_async_remote_copy(
            src_ref=s, dst_ref=d, send_sem=swap_send.at[i], recv_sem=swap_recv.at[i],
            device_id=partner, device_id_type=MESH,
        )
        for i, (s, d) in enumerate(swaps)
    ]
    for copy in swaps:
        copy.start()
    for i in range(2):
        loads[i].wait()
        swaps[i].wait()

    def halos(p):
        def message(k, src, dst, device):
            return pltpu.make_async_remote_copy(
                src_ref=src, dst_ref=dst, send_sem=halo_send.at[k], recv_sem=halo_recv.at[p, k],
                device_id=device, device_id_type=MESH,
            )

        e = E[p]
        own, rows = pl.ds(1, HX), pl.ds(8, BY)
        return [
            (has_up, has_down, message(0, e.at[:, :, HX, rows], e.at[:, :, 0, rows], up)),
            (has_down, has_up, message(1, e.at[1:3, :, 1, rows], e.at[1:3, :, HX + 1, rows], down)),
            (has_right, has_left, message(2, e.at[:, :, own, 23:24], e.at[:, :, own, 7:8], right)),
            (has_left, has_right, message(3, e.at[0, :, own, 8:9], e.at[0, :, own, 24:25], left)),
            (has_left, has_right, message(4, e.at[2, :, own, 8:9], e.at[2, :, own, 24:25], left)),
            (
                jnp.logical_and(has_up, has_left), jnp.logical_and(has_down, has_right),
                message(5, e.at[0, :, HX, 8:9], e.at[0, :, 0, 24:25], up_left),
            ),
            (
                jnp.logical_and(has_down, has_right), jnp.logical_and(has_up, has_left),
                message(6, e.at[1, :, 1, 23:24], e.at[1, :, HX + 1, 7:8], down_right),
            ),
        ]

    def start(messages):
        for receiver, _, copy in messages:
            @pl.when(receiver)
            def _(copy=copy):
                copy.start()

    def finish(messages):
        for receiver, sender, copy in messages:
            @pl.when(sender)
            def _(copy=copy):
                copy.wait_recv()

            @pl.when(receiver)
            def _(copy=copy):
                copy.wait_send()

    def first(k, src, dst, device):
        return pltpu.make_async_remote_copy(
            src_ref=src, dst_ref=dst, send_sem=first_send.at[k], recv_sem=first_recv.at[k],
            device_id=device, device_id_type=MESH,
        )

    own, rows = pl.ds(1, HX), pl.ds(8, BY)
    h_layers = [
        (has_up, has_down, first(0, H.at[1:3, :, HX, rows], H.at[1:3, :, 0, rows], up)),
        (has_right, has_left, first(1, H.at[0, :, own, 23:24], H.at[0, :, own, 7:8], right)),
        (has_right, has_left, first(2, H.at[2, :, own, 23:24], H.at[2, :, own, 7:8], right)),
    ]
    start(h_layers)
    start(halos(0))
    for i in range(2, 5):
        loads[i].wait()
        swaps[i].wait()
    for copy in loads[5:]:
        copy.wait()

    rates = [[], [], [], []]
    for m in range(NMAT):
        turning = jnp.full((8, 128), freq_ref[m], F32) * DT
        half_loss = jnp.full((8, 128), damp_ref[m], F32) * (0.5 * DT)
        denominator = 1.0 + half_loss
        rates[0].append((2.0 - turning * turning) / denominator)
        rates[1].append(-(1.0 - half_loss) / denominator)
        rates[2].append(jnp.full((8, 128), strength_ref[m], F32) * turning * turning / denominator)
        rates[3].append(1.0 / jnp.full((8, 128), eps_ref[m], F32))

    @pl.loop(0, HX)
    def _(i):
        for z in range(2):
            for j in range(2):
                cell = mat[z, i, 8 * j:8 * j + 8]
                for k in range(4):
                    value = jnp.where(cell == 1, rates[k][1], rates[k][0])
                    value = jnp.where(cell == 2, rates[k][2], value)
                    coef[k, z, i, 8 * j:8 * j + 8] = jnp.where(cell == 3, rates[k][3], value)

    finish(h_layers)

    lane = lax.broadcasted_iota(jnp.int32, (8, 128), 1)
    last_lane, first_lane = lane == 127, lane == 0

    def ahead_z(v):
        r0, r1 = (pltpu.roll(x, 127, 1) for x in v)
        return jnp.where(last_lane, r1, r0), jnp.where(last_lane, 0.0, r1)

    def behind_z(v):
        r0, r1 = (pltpu.roll(x, 1, 1) for x in v)
        return jnp.where(first_lane, 0.0, r0), jnp.where(first_lane, r0, r1)

    def magnetic(e, i, j, keep=None):
        r = pl.ds(8 * j, 8)
        r1 = pl.ds(8 * j + 1, 8)
        ex, ey, ez = ([e[d, z, i, r] for z in range(2)] for d in range(3))
        ex_z, ey_z = ahead_z(ex), ahead_z(ey)
        for z in range(2):
            hx = H[0, z, i, r] - DT * ((e[2, z, i, r1] - ez[z]) - (ey_z[z] - ey[z]))
            hz = H[2, z, i, r] - DT * ((e[1, z, i + 1, r] - ey[z]) - (e[0, z, i, r1] - ex[z]))
            H[0, z, i, r] = hx if keep is None else jnp.where(keep, hx, 0.0)
            H[2, z, i, r] = hz if keep is None else jnp.where(keep, hz, 0.0)
            if j > 0:
                hy = H[1, z, i, r] - DT * ((ex_z[z] - ex[z]) - (e[2, z, i + 1, r] - ez[z]))
                H[1, z, i, r] = hy if keep is None else jnp.where(keep, hy, 0.0)

    def electric(e, e_new, now_ref, old_ref, i, j):
        r = pl.ds(8 * j, 8)
        r1 = pl.ds(8 * j - 1, 8)
        s = pl.ds(8 * (j - 1), 8)
        hx, hy, hz = ([H[d, z, i, r] for z in range(2)] for d in range(3))
        hx_z, hy_z = behind_z(hx), behind_z(hy)
        for z in range(2):
            curl = (
                (hz[z] - H[2, z, i, r1]) - (hy[z] - hy_z[z]),
                (hx[z] - hx_z[z]) - (hz[z] - H[2, z, i - 1, r]),
                (hy[z] - H[1, z, i - 1, r]) - (hx[z] - H[0, z, i, r1]),
            )
            keep, back, drive, inverse = (coef[k, z, i - 1, s] for k in range(4))
            for d in range(3):
                value = e[d, z, i, r]
                now = now_ref[d, z, i - 1, s]
                new = keep * now + back * old_ref[d, z, i - 1, s] + drive * value
                old_ref[d, z, i - 1, s] = new
                e_new[d, z, i, r] = value + inverse * (DT * curl[d] - (new - now))

    def sample_copy(n, k, device):
        g, t = device
        return pltpu.make_async_remote_copy(
            src_ref=stage.at[n, t], dst_ref=samp.at[n], send_sem=samp_send.at[k], recv_sem=samp_recv.at[n],
            device_id=(g, gy, t), device_id_type=MESH,
        )

    receivers = [(NGX - 1, 0)]
    receivers += [(ROW * k + ROW - 1, t) for k in range(NGX // ROW - 1) for t in range(2)]
    receivers += [(NGX - ROW + k, t) for k in range(ROW - 1) for t in range(2)]

    def relay_copy(n, k):
        return pltpu.make_async_remote_copy(
            src_ref=samp.at[n], dst_ref=samp.at[n], send_sem=samp_send.at[k], recv_sem=samp_recv.at[n],
            device_id=(row_end - 1 - k, gy, c), device_id_type=MESH,
        )

    def relay(n):
        @pl.when(is_relay)
        def _():
            @pl.when(n > 0)
            def _():
                for k in range(ROW - 1):
                    relay_copy(n - 1, k).wait_send()

            relay_copy(n, 0).wait_recv()
            for k in range(ROW - 1):
                relay_copy(n, k).start()

    def start_next(n, p):
        @pl.when(n < STEPS - 1)
        def _():
            start(halos(p))

    def step(n, p):
        e, e_new = E[p], E[1 - p]
        now_ref, old_ref = (P0, P1) if p == 0 else (P1, P0)

        @pl.loop(0, 3)
        def _(b):
            for u in range(5):
                magnetic(e, 1 + 5 * b + u, 1)

        finish(halos(p))
        magnetic(e, 0, 1, has_down)
        magnetic(e, 0, 2, has_down)
        magnetic(e, HX, 1)

        @pl.loop(0, 2)
        def _(b):
            for u in range(8):
                magnetic(e, 1 + 8 * b + u, 0, has_left)
                magnetic(e, 1 + 8 * b + u, 2)

        @pl.loop(0, 4)
        def _(b):
            for u in range(4):
                electric(e, e_new, now_ref, old_ref, 1 + 4 * b + u, 1)
                electric(e, e_new, now_ref, old_ref, 1 + 4 * b + u, 2)

        start_next(n, 1 - p)

        @pl.when(n > 0)
        def _():
            relay(n - 1)

        @pl.when(is_holder)
        def _():
            @pl.when(n > 0)
            def _():
                for k, device in enumerate(receivers):
                    sample_copy(n - 1, k, device).wait_send()

            for t in range(2):
                for d in range(2):
                    stage[n, t, d] = e_new[d + 1, t, 1, 8:24]
                    stage[n, t, d + 2] = H[d + 1, t, 1, 8:24]
            for k, device in enumerate(receivers):
                sample_copy(n, k, device).start()
            samp[n] = stage[n, 1]

    @pl.loop(0, STEPS // 2)
    def _(b):
        step(2 * b, 0)
        step(2 * b + 1, 1)

    e_out = lambda z: (E0.at[:, z, own, rows], out_f.at[0:3, here])
    h_out = lambda z: (H.at[:, z, own, rows], out_f.at[3:6, here])
    p_out = lambda z: (P0.at[:, z], out_p.at[0, :, here])
    q_out = lambda z: (P1.at[:, z], out_p.at[1, :, here])
    sends = []
    for k, out in enumerate((e_out, h_out, p_out, q_out)):
        s, d = out(other)
        sends.append(pltpu.make_async_remote_copy(
            src_ref=s, dst_ref=d, send_sem=out_send.at[k], recv_sem=out_recv.at[k],
            device_id=partner, device_id_type=MESH,
        ))
        s, d = out(c)
        sends.append(pltpu.make_async_copy(s, d, out_sem.at[k]))
    for copy in sends:
        copy.start()

    relay(STEPS - 1)

    @pl.when(is_holder)
    def _():
        for k, device in enumerate(receivers):
            sample_copy(STEPS - 1, k, device).wait_send()

    @pl.when(jnp.logical_not(jnp.logical_or(is_holder, is_relay)))
    def _():
        for n in range(STEPS):
            sample_copy(n, 0, (0, 0)).wait_recv()

    rows_of = [samp[n].reshape(4 * BY, 128) for n in range(STEPS)]
    for f in range(2):
        real = weight_ref[0, 2 * gx + f] * rows_of[0]
        imag = weight_ref[0, NF + 2 * gx + f] * rows_of[0]
        for n in range(1, STEPS):
            real += weight_ref[n, 2 * gx + f] * rows_of[n]
            imag += weight_ref[n, NF + 2 * gx + f] * rows_of[n]
        both = jnp.concatenate([real, imag], axis=0)
        inner = jnp.dot(both, ztab[f], precision=HIGHEST, preferred_element_type=F32)
        inner_real = inner[:64, :128] - inner[64:, 128:]
        inner_imag = inner[:64, 128:] + inner[64:, :128]
        cos_y, sin_y = ytab[f, 0], ytab[f, 1]
        lines = []
        for d in range(4):
            re, im = inner_real[16 * d:16 * d + 16], inner_imag[16 * d:16 * d + 16]
            lines.append(jnp.sum(re * cos_y - im * sin_y, axis=0, keepdims=True))
            lines.append(jnp.sum(re * sin_y + im * cos_y, axis=0, keepdims=True))
        part[f] = jnp.concatenate(lines, axis=0)

    far = []
    for k in range(1, NGY * NAF):
        them = lax.rem(me + k, NGY * NAF)
        far.append(pltpu.make_async_remote_copy(
            src_ref=part.at[them // 4], dst_ref=parts.at[k], send_sem=far_send.at[k], recv_sem=far_recv.at[k],
            device_id=(gx, them // NAF, lax.rem(them, NAF)), device_id_type=MESH,
        ))
    for copy in far:
        copy.start()

    mine = (owner_ref[...] == gx).astype(F32)
    row = lax.broadcasted_iota(jnp.int32, (64, 64), 0)
    col = lax.broadcasted_iota(jnp.int32, (64, 64), 1)
    rank = jnp.dot(
        jnp.broadcast_to(mine, (8, 64)), (row < col).astype(F32), precision=HIGHEST, preferred_element_type=F32
    )
    slot = lax.broadcasted_iota(jnp.int32, (8, 64), 0).astype(F32)
    picked = jnp.where(rank == slot, mine, 0.0)
    chosen = [
        jnp.dot(picked, rows_of[n], precision=HIGHEST, preferred_element_type=F32) for n in range(STEPS)
    ]
    for s in range(SLOTS):
        for k in range(2 * NF // 8):
            total = spread[0, 8 * k:8 * k + 8] * chosen[0][s:s + 1]
            for n in range(1, STEPS):
                total += spread[n, 8 * k:8 * k + 8] * chosen[n][s:s + 1]
            out_s[0, 0, 0, s, 8 * k:8 * k + 8] = total

    total = part[me // 4]
    for k in range(1, NGY * NAF):
        far[k - 1].wait()
        total += parts[k]
    block = lax.rem(me, 4)
    total = pltpu.roll(total, lax.rem(128 - 32 * block, 128), 1)
    out_far[...] = total[:, :32]
    for copy in sends:
        copy.wait()

    @pl.when(is_relay)
    def _():
        for k in range(ROW - 1):
            relay_copy(STEPS - 1, k).wait_send()


def on_device(constants, fields, polarization, material, eps_inf, pole_strength, pole_freq, damping, owner):
    weights, spread, z_table, y_table = constants
    smem = pl.BlockSpec(memory_space=pltpu.SMEM)
    vmem = pl.BlockSpec(memory_space=pltpu.VMEM)
    hbm = pl.BlockSpec(memory_space=pl.ANY)
    dma = lambda *shape: pltpu.SemaphoreType.DMA(shape)
    return pl.pallas_call(
        kernel,
        out_shape=(
            pltpu.VMEM(fields.shape, F32),
            pltpu.VMEM(polarization.shape, F32),
            pltpu.VMEM((1, 1, 1, SLOTS, 2 * NF, BZ), F32),
            pltpu.VMEM((8, 32), F32),
        ),
        in_specs=[smem] * 5 + [vmem] + [hbm] * 6,
        out_specs=(vmem, vmem, vmem, vmem),
        scratch_shapes=[
            pltpu.VMEM((3, 2, HX + 2, 32, 128), F32),
            pltpu.VMEM((3, 2, HX + 2, 32, 128), F32),
            pltpu.VMEM((3, 2, HX + 1, 24, 128), F32),
            pltpu.VMEM((3, 2, HX, BY, 128), F32),
            pltpu.VMEM((3, 2, HX, BY, 128), F32),
            pltpu.VMEM((2, HX, BY, 128), jnp.int32),
            pltpu.VMEM((4, 2, HX, BY, 128), F32),
            pltpu.VMEM((STEPS, 2, 4, BY, 128), F32),
            pltpu.VMEM((STEPS, 4, BY, 128), F32),
            pltpu.VMEM((2, BZ, 2 * NANG), F32),
            pltpu.VMEM((2, 2, BY, NANG), F32),
            pltpu.VMEM((STEPS, 2 * NF, 128), F32),
            pltpu.VMEM((2, 8, 128), F32),
            pltpu.VMEM((8, 8, 128), F32),
            dma(8), dma(5), dma(5), dma(7), dma(2, 7), dma(3), dma(3),
            dma(13), dma(STEPS), dma(8), dma(8), dma(4), dma(4), dma(4),
        ],
        compiler_params=pltpu.CompilerParams(
            collective_id=0, has_side_effects=True, vmem_limit_bytes=56 << 20
        ),
        name="fdtd",
    )(
        eps_inf, pole_strength, pole_freq, damping, weights, owner.reshape(1, 64),
        fields, polarization, material, spread, z_table, y_table,
    )


def solution(mesh):
    constants = tables()

    def whole(*arguments):
        return on_device(tuple(jnp.asarray(x) for x in constants), *arguments)

    return jax.shard_map(
        whole,
        mesh=mesh,
        in_specs=(
            P(None, "gx", "gy", "af"),
            P(None, None, "gx", "gy", "af"),
            P("gx", "gy", "af"),
            P(), P(), P(), P(),
            P("gy", "af", None, None),
        ),
        out_specs=(
            P(None, "gx", "gy", "af"),
            P(None, None, "gx", "gy", "af"),
            P("gx", "gy", "af", None, None, None),
            P(None, ("gx", "gy", "af")),
        ),
        check_vma=False,
    )
```

```python
import functools
import math

import jax
import jax.numpy as jnp
import numpy as np
from jax import lax
from jax.experimental import pallas as pl
from jax.experimental.pallas import tpu as pltpu
from jax.sharding import PartitionSpec as P

STEPS = 8
NF = 32
NANG = 128
NMAT = 4
NGX, NGY, NAF = 16, 4, 2
BX, BY, BZ = 32, 16, 128
HX = BX // 2
ROW = 4
SLOTS = 8
DT = 0.5
MESH = pl.DeviceIdType.MESH
HIGHEST = lax.Precision.HIGHEST
F32 = jnp.float32


def tables():
    omega = 0.25 + 1.5 * np.arange(NF) / NF
    t = (np.arange(STEPS) + 1.0) * DT
    phase = t[:, None] * omega[None, :]
    weights = np.concatenate([np.cos(phase), -np.sin(phase)], axis=1) / STEPS
    angle = np.arange(NANG)
    rho = 0.25 + 0.7 * (angle + 0.5) / NANG
    s_y = rho * np.cos(2.0 * np.pi * angle / NANG)
    s_z = rho * np.sin(2.0 * np.pi * angle / NANG)
    z_phase = omega[:, None, None] * s_z[None, None, :] * np.arange(BZ)[None, :, None]
    z_table = np.concatenate([np.cos(z_phase), np.sin(z_phase)], axis=2)
    z_table = z_table.reshape(NGX, 2, BZ, 2 * NANG)
    y = np.arange(NGY * BY).reshape(NGY, 1, BY)
    z0 = (BZ * np.arange(NAF)).reshape(1, NAF, 1)
    shift = s_y * y[..., None] + s_z * z0[..., None]
    y_phase = omega[:, None, None] * shift[:, :, None]
    y_table = np.stack([np.cos(y_phase), np.sin(y_phase)], axis=3)
    y_table = y_table / math.sqrt(NGY * BY * NAF * BZ)
    y_table = y_table.reshape(NGY * NAF, NGX, 2, 2, BY, NANG)
    spread = np.broadcast_to(weights[:, :, None], (STEPS, 2 * NF, 128))
    return (
        weights.astype(np.float32),
        spread.astype(np.float32),
        z_table.astype(np.float32),
        y_table.astype(np.float32),
    )


def kernel(
    eps_ref, strength_ref, freq_ref, damp_ref, weight_ref, owner_ref,
    fields_ref, pol_ref, mat_ref, spread_hbm, ztab_hbm, ytab_hbm,
    out_f, out_p, out_s, out_far,
    E0, E1, H, P0, P1, mat, coef, stage, samp, ztab, ytab, spread, sums, part, parts,
    local_sem, swap_send, swap_recv, halo_send, halo_recv, first_send, first_recv,
    samp_send, samp_recv, far_send, far_recv, out_sem, out_send, out_recv,
):
    gx, gy, c = lax.axis_index("gx"), lax.axis_index("gy"), lax.axis_index("af")
    place = 2 * gx + c
    E = (E0, E1)
    other = 1 - c
    has_up, has_down = place < 2 * NGX - 1, place > 0
    has_right, has_left = gy < NGY - 1, gy > 0
    up = (gx + c, gy, other)
    down = (gx - other, gy, other)
    right, left = (gx, gy + 1, c), (gx, gy - 1, c)
    up_left = (gx + c, gy - 1, other)
    down_right = (gx - other, gy + 1, other)
    partner = (gx, gy, other)
    is_holder = jnp.logical_and(gx == NGX - 1, c == 1)
    row_end = gx // ROW * ROW + ROW - 1
    is_last_row = gx // ROW == NGX // ROW - 1
    is_relay = jnp.logical_and(gx == row_end, jnp.logical_not(is_last_row))
    fed_by_relay = jnp.logical_and(gx != row_end, jnp.logical_not(is_last_row))
    fed_by_holder = jnp.logical_or(is_relay, jnp.logical_and(is_last_row, gx != row_end))
    me = gy * NAF + c

    barrier = pltpu.get_barrier_semaphore()

    def greet(device):
        pl.semaphore_signal(barrier, inc=1, device_id=device, device_id_type=MESH)

    for k in range(1, NGY * NAF):
        them = lax.rem(me + k, NGY * NAF)
        greet((gx, them // NAF, lax.rem(them, NAF)))
    across_up = jnp.logical_and(c == 1, has_up)
    across_down = jnp.logical_and(c == 0, has_down)
    across_up_left = jnp.logical_and(across_up, has_left)
    across_down_right = jnp.logical_and(across_down, has_right)
    for there, device in (
        (across_up, up), (across_down, down), (across_up_left, up_left), (across_down_right, down_right),
    ):
        @pl.when(there)
        def _(device=device):
            greet(device)

    @pl.when(fed_by_relay)
    def _():
        greet((row_end, gy, c))

    @pl.when(fed_by_holder)
    def _():
        greet((NGX - 1, gy, 1))

    here = pl.ds(c * HX, HX)
    there = pl.ds(other * HX, HX)
    loads = [
        (fields_ref.at[0:3, here], E0.at[:, c, 1:HX + 1, 8:24]),
        (fields_ref.at[3:6, here], H.at[:, c, 1:HX + 1, 8:24]),
        (pol_ref.at[0, :, here], P0.at[:, c]),
        (pol_ref.at[1, :, here], P1.at[:, c]),
        (mat_ref.at[here], mat.at[c]),
        (ztab_hbm.at[gx], ztab),
        (ytab_hbm.at[me, gx], ytab),
        (spread_hbm, spread),
    ]
    loads = [pltpu.make_async_copy(s, d, local_sem.at[i]) for i, (s, d) in enumerate(loads)]
    for copy in loads:
        copy.start()

    @pl.when(jnp.logical_not(has_up))
    def _():
        for p in range(2):
            for d in (1, 2):
                for z in range(2):
                    E[p][d, z, HX + 1, 0:24] = jnp.zeros((24, 128), F32)

    @pl.when(jnp.logical_not(has_right))
    def _():
        @pl.loop(0, HX + 1)
        def _(i):
            for p in range(2):
                for d in (0, 2):
                    for z in range(2):
                        E[p][d, z, i, 24:32] = jnp.zeros((8, 128), F32)

    count = (
        NGY * NAF - 1
        + across_up.astype(jnp.int32) + across_down.astype(jnp.int32)
        + across_up_left.astype(jnp.int32) + across_down_right.astype(jnp.int32)
        + jnp.where(is_holder, 2 * (NGX // ROW + ROW - 2), 0)
        + jnp.where(is_relay, ROW - 1, 0)
    )
    pl.semaphore_wait(barrier, count)

    swaps = [
        (fields_ref.at[0:3, there], E0.at[:, c, 1:HX + 1, 8:24]),
        (fields_ref.at[3:6, there], H.at[:, c, 1:HX + 1, 8:24]),
        (pol_ref.at[0, :, there], P0.at[:, c]),
        (pol_ref.at[1, :, there], P1.at[:, c]),
        (mat_ref.at[there], mat.at[c]),
    ]
    swaps = [
        pltpu.make_async_remote_copy(
            src_ref=s, dst_ref=d, send_sem=swap_send.at[i], recv_sem=swap_recv.at[i],
            device_id=partner, device_id_type=MESH,
        )
        for i, (s, d) in enumerate(swaps)
    ]
    for copy in swaps:
        copy.start()

    def halos(p):
        def message(k, src, dst, device):
            return pltpu.make_async_remote_copy(
                src_ref=src, dst_ref=dst, send_sem=halo_send.at[k], recv_sem=halo_recv.at[p, k],
                device_id=device, device_id_type=MESH,
            )

        e = E[p]
        own, rows = pl.ds(1, HX), pl.ds(8, BY)
        along_x = [
            (has_up, has_down, message(0, e.at[:, :, HX, rows], e.at[:, :, 0, rows], up)),
            (has_down, has_up, message(1, e.at[1:3, :, 1, rows], e.at[1:3, :, HX + 1, rows], down)),
            (
                jnp.logical_and(has_up, has_left), jnp.logical_and(has_down, has_right),
                message(5, e.at[0, :, HX, 8:9], e.at[0, :, 0, 24:25], up_left),
            ),
            (
                jnp.logical_and(has_down, has_right), jnp.logical_and(has_up, has_left),
                message(6, e.at[1, :, 1, 23:24], e.at[1, :, HX + 1, 7:8], down_right),
            ),
        ]
        along_y = [
            (has_right, has_left, message(2, e.at[:, :, own, 23:24], e.at[:, :, own, 7:8], right)),
            (has_left, has_right, message(3, e.at[0, :, own, 8:9], e.at[0, :, own, 24:25], left)),
            (has_left, has_right, message(4, e.at[2, :, own, 8:9], e.at[2, :, own, 24:25], left)),
        ]
        return along_y, along_x

    def start(messages):
        for receiver, _, copy in messages:
            @pl.when(receiver)
            def _(copy=copy):
                copy.start()

    def finish(messages):
        for receiver, sender, copy in messages:
            @pl.when(sender)
            def _(copy=copy):
                copy.wait_recv()

            @pl.when(receiver)
            def _(copy=copy):
                copy.wait_send()

    def first(k, src, dst, device):
        return pltpu.make_async_remote_copy(
            src_ref=src, dst_ref=dst, send_sem=first_send.at[k], recv_sem=first_recv.at[k],
            device_id=device, device_id_type=MESH,
        )

    own, rows = pl.ds(1, HX), pl.ds(8, BY)
    h_layers = [
        (has_up, has_down, first(0, H.at[1:3, :, HX, rows], H.at[1:3, :, 0, rows], up)),
        (has_right, has_left, first(1, H.at[0, :, own, 23:24], H.at[0, :, own, 7:8], right)),
        (has_right, has_left, first(2, H.at[2, :, own, 23:24], H.at[2, :, own, 7:8], right)),
    ]
    along_y, along_x = halos(0)
    loads[0].wait()
    swaps[0].wait()
    start(along_x)
    start(along_y)
    loads[1].wait()
    swaps[1].wait()
    start(h_layers)
    for i in range(2, 5):
        loads[i].wait()
        swaps[i].wait()
    for copy in loads[5:]:
        copy.wait()

    rates = [[], [], [], []]
    for m in range(NMAT):
        turning = jnp.full((8, 128), freq_ref[m], F32) * DT
        half_loss = jnp.full((8, 128), damp_ref[m], F32) * (0.5 * DT)
        denominator = 1.0 + half_loss
        rates[0].append((2.0 - turning * turning) / denominator)
        rates[1].append(-(1.0 - half_loss) / denominator)
        rates[2].append(jnp.full((8, 128), strength_ref[m], F32) * turning * turning / denominator)
        rates[3].append(1.0 / jnp.full((8, 128), eps_ref[m], F32))

    @pl.loop(0, HX)
    def _(i):
        for z in range(2):
            for j in range(2):
                cell = mat[z, i, 8 * j:8 * j + 8]
                for k in range(4):
                    value = jnp.where(cell == 1, rates[k][1], rates[k][0])
                    value = jnp.where(cell == 2, rates[k][2], value)
                    coef[k, z, i, 8 * j:8 * j + 8] = jnp.where(cell == 3, rates[k][3], value)

    finish(h_layers)

    lane = lax.broadcasted_iota(jnp.int32, (8, 128), 1)
    last_lane, first_lane = lane == 127, lane == 0

    def ahead_z(v):
        r0, r1 = (pltpu.roll(x, 127, 1) for x in v)
        return jnp.where(last_lane, r1, r0), jnp.where(last_lane, 0.0, r1)

    def behind_z(v):
        r0, r1 = (pltpu.roll(x, 1, 1) for x in v)
        return jnp.where(first_lane, 0.0, r0), jnp.where(first_lane, r0, r1)

    def magnetic(e, i, j, keep=None):
        r = pl.ds(8 * j, 8)
        r1 = pl.ds(8 * j + 1, 8)
        ex, ey, ez = ([e[d, z, i, r] for z in range(2)] for d in range(3))
        ex_z, ey_z = ahead_z(ex), ahead_z(ey)
        for z in range(2):
            hx = H[0, z, i, r] - DT * ((e[2, z, i, r1] - ez[z]) - (ey_z[z] - ey[z]))
            hz = H[2, z, i, r] - DT * ((e[1, z, i + 1, r] - ey[z]) - (e[0, z, i, r1] - ex[z]))
            H[0, z, i, r] = hx if keep is None else jnp.where(keep, hx, 0.0)
            H[2, z, i, r] = hz if keep is None else jnp.where(keep, hz, 0.0)
            if j > 0:
                hy = H[1, z, i, r] - DT * ((ex_z[z] - ex[z]) - (e[2, z, i + 1, r] - ez[z]))
                H[1, z, i, r] = hy if keep is None else jnp.where(keep, hy, 0.0)

    def electric(e, e_new, now_ref, old_ref, i, j):
        r = pl.ds(8 * j, 8)
        r1 = pl.ds(8 * j - 1, 8)
        s = pl.ds(8 * (j - 1), 8)
        hx, hy, hz = ([H[d, z, i, r] for z in range(2)] for d in range(3))
        hx_z, hy_z = behind_z(hx), behind_z(hy)
        for z in range(2):
            curl = (
                (hz[z] - H[2, z, i, r1]) - (hy[z] - hy_z[z]),
                (hx[z] - hx_z[z]) - (hz[z] - H[2, z, i - 1, r]),
                (hy[z] - H[1, z, i - 1, r]) - (hx[z] - H[0, z, i, r1]),
            )
            keep, back, drive, inverse = (coef[k, z, i - 1, s] for k in range(4))
            for d in range(3):
                value = e[d, z, i, r]
                now = now_ref[d, z, i - 1, s]
                new = keep * now + back * old_ref[d, z, i - 1, s] + drive * value
                old_ref[d, z, i - 1, s] = new
                e_new[d, z, i, r] = value + inverse * (DT * curl[d] - (new - now))

    def sample_copy(n, k, device):
        g, t = device
        return pltpu.make_async_remote_copy(
            src_ref=stage.at[n, t], dst_ref=samp.at[n], send_sem=samp_send.at[k], recv_sem=samp_recv.at[n],
            device_id=(g, gy, t), device_id_type=MESH,
        )

    receivers = [(NGX - 1, 0)]
    receivers += [(ROW * k + ROW - 1, t) for k in range(NGX // ROW - 1) for t in range(2)]
    receivers += [(NGX - ROW + k, t) for k in range(ROW - 1) for t in range(2)]

    def relay_copy(n, k):
        return pltpu.make_async_remote_copy(
            src_ref=samp.at[n], dst_ref=samp.at[n], send_sem=samp_send.at[k], recv_sem=samp_recv.at[n],
            device_id=(row_end - 1 - k, gy, c), device_id_type=MESH,
        )

    def relay(n):
        @pl.when(is_relay)
        def _():
            @pl.when(n > 0)
            def _():
                for k in range(ROW - 1):
                    relay_copy(n - 1, k).wait_send()

            relay_copy(n, 0).wait_recv()
            for k in range(ROW - 1):
                relay_copy(n, k).start()

    def start_next(n, p):
        @pl.when(n < STEPS - 1)
        def _():
            along_y, along_x = halos(p)
            start(along_x)
            start(along_y)

    def step(n, p):
        e, e_new = E[p], E[1 - p]
        now_ref, old_ref = (P0, P1) if p == 0 else (P1, P0)

        along_y, along_x = halos(p)

        @pl.loop(0, 3)
        def _(b):
            for u in range(5):
                magnetic(e, 1 + 5 * b + u, 1)

        finish(along_y)

        @pl.loop(0, 3)
        def _(b):
            for u in range(5):
                magnetic(e, 1 + 5 * b + u, 0, has_left)
                magnetic(e, 1 + 5 * b + u, 2)

        @pl.loop(0, 2)
        def _(b):
            for u in range(7):
                electric(e, e_new, now_ref, old_ref, 2 + 7 * b + u, 1)
                electric(e, e_new, now_ref, old_ref, 2 + 7 * b + u, 2)

        finish(along_x)
        magnetic(e, 0, 1, has_down)
        magnetic(e, 0, 2, has_down)
        magnetic(e, HX, 0, has_left)
        for j in (1, 2):
            magnetic(e, HX, j)
        for i in (1, HX):
            for j in (1, 2):
                electric(e, e_new, now_ref, old_ref, i, j)

        start_next(n, 1 - p)

        @pl.when(n > 0)
        def _():
            relay(n - 1)

        @pl.when(is_holder)
        def _():
            @pl.when(n > 0)
            def _():
                for k, device in enumerate(receivers):
                    sample_copy(n - 1, k, device).wait_send()

            for t in range(2):
                for d in range(2):
                    stage[n, t, d] = e_new[d + 1, t, 1, 8:24]
                    stage[n, t, d + 2] = H[d + 1, t, 1, 8:24]
            for k, device in enumerate(receivers):
                sample_copy(n, k, device).start()
            samp[n] = stage[n, 1]

    @pl.loop(0, STEPS // 2)
    def _(b):
        step(2 * b, 0)
        step(2 * b + 1, 1)

    e_out = lambda z: (E0.at[:, z, own, rows], out_f.at[0:3, here])
    h_out = lambda z: (H.at[:, z, own, rows], out_f.at[3:6, here])
    p_out = lambda z: (P0.at[:, z], out_p.at[0, :, here])
    q_out = lambda z: (P1.at[:, z], out_p.at[1, :, here])
    sends = []
    for k, out in enumerate((e_out, h_out, p_out, q_out)):
        s, d = out(other)
        sends.append(pltpu.make_async_remote_copy(
            src_ref=s, dst_ref=d, send_sem=out_send.at[k], recv_sem=out_recv.at[k],
            device_id=partner, device_id_type=MESH,
        ))
        s, d = out(c)
        sends.append(pltpu.make_async_copy(s, d, out_sem.at[k]))
    for copy in sends:
        copy.start()

    last = STEPS - 1
    is_end = jnp.logical_not(jnp.logical_or(is_holder, is_relay))

    @pl.when(is_end)
    def _():
        for n in range(last):
            sample_copy(n, 0, (0, 0)).wait_recv()

    def sample(n):
        return samp[n].reshape(4 * BY, 128)

    def weight(n, f):
        return weight_ref[n, 2 * gx + f], weight_ref[n, NF + 2 * gx + f]

    for f in range(2):
        for k in range(2):
            total = weight(0, f)[k] * sample(0)
            for n in range(1, last):
                total += weight(n, f)[k] * sample(n)
            sums[f, 64 * k:64 * k + 64] = total

    mine = (owner_ref[...] == gx).astype(F32)
    row = lax.broadcasted_iota(jnp.int32, (64, 64), 0)
    col = lax.broadcasted_iota(jnp.int32, (64, 64), 1)
    rank = jnp.dot(
        jnp.broadcast_to(mine, (8, 64)), (row < col).astype(F32), precision=HIGHEST, preferred_element_type=F32
    )
    slot = lax.broadcasted_iota(jnp.int32, (8, 64), 0).astype(F32)
    picked = jnp.where(rank == slot, mine, 0.0)

    def choose(n):
        return jnp.dot(picked, sample(n), precision=HIGHEST, preferred_element_type=F32)

    chosen = [choose(n) for n in range(last)]
    for s in range(SLOTS):
        for k in range(2 * NF // 8):
            total = spread[0, 8 * k:8 * k + 8] * chosen[0][s:s + 1]
            for n in range(1, last):
                total += spread[n, 8 * k:8 * k + 8] * chosen[n][s:s + 1]
            out_s[0, 0, 0, s, 8 * k:8 * k + 8] = total

    relay(last)

    @pl.when(is_end)
    def _():
        sample_copy(last, 0, (0, 0)).wait_recv()

    for f in range(2):
        for k in range(2):
            sums[f, 64 * k:64 * k + 64] += weight(last, f)[k] * sample(last)
        inner = jnp.dot(sums[f], ztab[f], precision=HIGHEST, preferred_element_type=F32)
        inner_real = inner[:64, :128] - inner[64:, 128:]
        inner_imag = inner[:64, 128:] + inner[64:, :128]
        cos_y, sin_y = ytab[f, 0], ytab[f, 1]
        lines = []
        for d in range(4):
            re, im = inner_real[16 * d:16 * d + 16], inner_imag[16 * d:16 * d + 16]
            lines.append(jnp.sum(re * cos_y - im * sin_y, axis=0, keepdims=True))
            lines.append(jnp.sum(re * sin_y + im * cos_y, axis=0, keepdims=True))
        part[f] = jnp.concatenate(lines, axis=0)

    far = []
    for k in range(1, NGY * NAF):
        them = lax.rem(me + k, NGY * NAF)
        far.append(pltpu.make_async_remote_copy(
            src_ref=part.at[them // 4], dst_ref=parts.at[k], send_sem=far_send.at[k], recv_sem=far_recv.at[k],
            device_id=(gx, them // NAF, lax.rem(them, NAF)), device_id_type=MESH,
        ))
    for copy in far:
        copy.start()

    chosen = choose(last)
    for s in range(SLOTS):
        for k in range(2 * NF // 8):
            out_s[0, 0, 0, s, 8 * k:8 * k + 8] += spread[last, 8 * k:8 * k + 8] * chosen[s:s + 1]

    total = part[me // 4]
    for k in range(1, NGY * NAF):
        far[k - 1].wait()
        total += parts[k]
    block = lax.rem(me, 4)
    total = pltpu.roll(total, lax.rem(128 - 32 * block, 128), 1)
    out_far[...] = total[:, :32]
    for copy in sends:
        copy.wait()

    @pl.when(is_holder)
    def _():
        for k, device in enumerate(receivers):
            sample_copy(last, k, device).wait_send()

    @pl.when(is_relay)
    def _():
        for k in range(ROW - 1):
            relay_copy(last, k).wait_send()


def on_device(constants, fields, polarization, material, eps_inf, pole_strength, pole_freq, damping, owner):
    weights, spread, z_table, y_table = constants
    smem = pl.BlockSpec(memory_space=pltpu.SMEM)
    vmem = pl.BlockSpec(memory_space=pltpu.VMEM)
    hbm = pl.BlockSpec(memory_space=pl.ANY)
    dma = lambda *shape: pltpu.SemaphoreType.DMA(shape)
    return pl.pallas_call(
        kernel,
        out_shape=(
            pltpu.VMEM(fields.shape, F32),
            pltpu.VMEM(polarization.shape, F32),
            pltpu.VMEM((1, 1, 1, SLOTS, 2 * NF, BZ), F32),
            pltpu.VMEM((8, 32), F32),
        ),
        in_specs=[smem] * 5 + [vmem] + [hbm] * 6,
        out_specs=(vmem, vmem, vmem, vmem),
        scratch_shapes=[
            pltpu.VMEM((3, 2, HX + 2, 32, 128), F32),
            pltpu.VMEM((3, 2, HX + 2, 32, 128), F32),
            pltpu.VMEM((3, 2, HX + 1, 24, 128), F32),
            pltpu.VMEM((3, 2, HX, BY, 128), F32),
            pltpu.VMEM((3, 2, HX, BY, 128), F32),
            pltpu.VMEM((2, HX, BY, 128), jnp.int32),
            pltpu.VMEM((4, 2, HX, BY, 128), F32),
            pltpu.VMEM((STEPS, 2, 4, BY, 128), F32),
            pltpu.VMEM((STEPS, 4, BY, 128), F32),
            pltpu.VMEM((2, BZ, 2 * NANG), F32),
            pltpu.VMEM((2, 2, BY, NANG), F32),
            pltpu.VMEM((STEPS, 2 * NF, 128), F32),
            pltpu.VMEM((2, 128, 128), F32),
            pltpu.VMEM((2, 8, 128), F32),
            pltpu.VMEM((8, 8, 128), F32),
            dma(8), dma(5), dma(5), dma(7), dma(2, 7), dma(3), dma(3),
            dma(13), dma(STEPS), dma(8), dma(8), dma(4), dma(4), dma(4),
        ],
        compiler_params=pltpu.CompilerParams(
            collective_id=0, has_side_effects=True, vmem_limit_bytes=56 << 20
        ),
        name="fdtd",
    )(
        eps_inf, pole_strength, pole_freq, damping, weights, owner.reshape(1, 64),
        fields, polarization, material, spread, z_table, y_table,
    )


def solution(mesh):
    constants = tables()

    def whole(*arguments):
        return on_device(tuple(jnp.asarray(x) for x in constants), *arguments)

    return jax.shard_map(
        whole,
        mesh=mesh,
        in_specs=(
            P(None, "gx", "gy", "af"),
            P(None, None, "gx", "gy", "af"),
            P("gx", "gy", "af"),
            P(), P(), P(), P(),
            P("gy", "af", None, None),
        ),
        out_specs=(
            P(None, "gx", "gy", "af"),
            P(None, None, "gx", "gy", "af"),
            P("gx", "gy", "af", None, None, None),
            P(None, ("gx", "gy", "af")),
        ),
        check_vma=False,
    )
```

```python
import functools
import math

import jax
import jax.numpy as jnp
import numpy as np
from jax import lax
from jax.experimental import pallas as pl
from jax.experimental.pallas import tpu as pltpu
from jax.sharding import PartitionSpec as P

STEPS = 8
NF = 32
NANG = 128
NMAT = 4
NGX, NGY, NAF = 16, 4, 2
BX, BY, BZ = 32, 16, 128
HX = BX // 2
ROW = 4
SLOTS = 8
DT = 0.5
MESH = pl.DeviceIdType.MESH
HIGHEST = lax.Precision.HIGHEST
F32 = jnp.float32


def tables():
    omega = 0.25 + 1.5 * np.arange(NF) / NF
    t = (np.arange(STEPS) + 1.0) * DT
    phase = t[:, None] * omega[None, :]
    weights = np.concatenate([np.cos(phase), -np.sin(phase)], axis=1) / STEPS
    angle = np.arange(NANG)
    rho = 0.25 + 0.7 * (angle + 0.5) / NANG
    s_y = rho * np.cos(2.0 * np.pi * angle / NANG)
    s_z = rho * np.sin(2.0 * np.pi * angle / NANG)
    z_phase = omega[:, None, None] * s_z[None, None, :] * np.arange(BZ)[None, :, None]
    z_table = np.concatenate([np.cos(z_phase), np.sin(z_phase)], axis=2)
    z_table = z_table.reshape(NGX, 2, BZ, 2 * NANG)
    y = np.arange(NGY * BY).reshape(NGY, 1, BY)
    z0 = (BZ * np.arange(NAF)).reshape(1, NAF, 1)
    shift = s_y * y[..., None] + s_z * z0[..., None]
    y_phase = omega[:, None, None] * shift[:, :, None]
    y_table = np.stack([np.cos(y_phase), np.sin(y_phase)], axis=3)
    y_table = y_table / math.sqrt(NGY * BY * NAF * BZ)
    y_table = y_table.reshape(NGY * NAF, NGX, 2, 2, BY, NANG)
    spread = np.broadcast_to(weights[:, :, None], (STEPS, 2 * NF, 128))
    return (
        weights.astype(np.float32),
        spread.astype(np.float32),
        z_table.astype(np.float32),
        y_table.astype(np.float32),
    )


def kernel(
    eps_ref, strength_ref, freq_ref, damp_ref, weight_ref, owner_ref,
    fields_ref, pol_ref, mat_ref, spread_hbm, ztab_hbm, ytab_hbm,
    out_f, out_p, out_s, out_far,
    E0, E1, H, P0, P1, mat, coef, stage, samp, ztab, ytab, spread, sums, part, parts,
    local_sem, swap_send, swap_recv, halo_send, halo_recv, first_send, first_recv,
    samp_send, samp_recv, far_send, far_recv, out_sem, out_send, out_recv,
):
    gx, gy, c = lax.axis_index("gx"), lax.axis_index("gy"), lax.axis_index("af")
    place = 2 * gx + c
    E = (E0, E1)
    other = 1 - c
    has_up, has_down = place < 2 * NGX - 1, place > 0
    has_right, has_left = gy < NGY - 1, gy > 0
    up = (gx + c, gy, other)
    down = (gx - other, gy, other)
    right, left = (gx, gy + 1, c), (gx, gy - 1, c)
    up_left = (gx + c, gy - 1, other)
    down_right = (gx - other, gy + 1, other)
    partner = (gx, gy, other)
    is_holder = jnp.logical_and(gx == NGX - 1, c == 1)
    row_end = gx // ROW * ROW + ROW - 1
    is_last_row = gx // ROW == NGX // ROW - 1
    is_relay = jnp.logical_and(jnp.logical_and(gx == row_end, c == 1), jnp.logical_not(is_last_row))
    fed_by_relay = jnp.logical_and(gx != row_end, jnp.logical_not(is_last_row))
    fed_by_holder = jnp.logical_or(is_relay, jnp.logical_and(is_last_row, gx != row_end))
    me = gy * NAF + c

    barrier = pltpu.get_barrier_semaphore()

    def greet(device):
        pl.semaphore_signal(barrier, inc=1, device_id=device, device_id_type=MESH)

    for k in range(1, NGY * NAF):
        them = lax.rem(me + k, NGY * NAF)
        greet((gx, them // NAF, lax.rem(them, NAF)))
    across_up = jnp.logical_and(c == 1, has_up)
    across_down = jnp.logical_and(c == 0, has_down)
    across_up_left = jnp.logical_and(across_up, has_left)
    across_down_right = jnp.logical_and(across_down, has_right)
    for there, device in (
        (across_up, up), (across_down, down), (across_up_left, up_left), (across_down_right, down_right),
    ):
        @pl.when(there)
        def _(device=device):
            greet(device)

    @pl.when(fed_by_relay)
    def _():
        greet((row_end, gy, 1))

    @pl.when(fed_by_holder)
    def _():
        greet((NGX - 1, gy, 1))

    here = pl.ds(c * HX, HX)
    there = pl.ds(other * HX, HX)
    loads = [
        (fields_ref.at[0:3, here], E0.at[:, c, 1:HX + 1, 8:24]),
        (fields_ref.at[3:6, here], H.at[:, c, 1:HX + 1, 8:24]),
        (pol_ref.at[0, :, here], P0.at[:, c]),
        (pol_ref.at[1, :, here], P1.at[:, c]),
        (mat_ref.at[here], mat.at[c]),
        (ztab_hbm.at[gx], ztab),
        (ytab_hbm.at[me, gx], ytab),
        (spread_hbm, spread),
    ]
    loads = [pltpu.make_async_copy(s, d, local_sem.at[i]) for i, (s, d) in enumerate(loads)]
    for copy in loads:
        copy.start()

    @pl.when(jnp.logical_not(has_up))
    def _():
        for p in range(2):
            for d in (1, 2):
                for z in range(2):
                    E[p][d, z, HX + 1, 0:24] = jnp.zeros((24, 128), F32)

    @pl.when(jnp.logical_not(has_right))
    def _():
        @pl.loop(0, HX + 1)
        def _(i):
            for p in range(2):
                for d in (0, 2):
                    for z in range(2):
                        E[p][d, z, i, 24:32] = jnp.zeros((8, 128), F32)

    count = (
        NGY * NAF - 1
        + across_up.astype(jnp.int32) + across_down.astype(jnp.int32)
        + across_up_left.astype(jnp.int32) + across_down_right.astype(jnp.int32)
        + jnp.where(is_holder, NGX // ROW - 1 + 2 * (ROW - 1), 0)
        + jnp.where(is_relay, 2 * (ROW - 1), 0)
    )
    pl.semaphore_wait(barrier, count)

    swaps = [
        (fields_ref.at[0:3, there], E0.at[:, c, 1:HX + 1, 8:24]),
        (fields_ref.at[3:6, there], H.at[:, c, 1:HX + 1, 8:24]),
        (pol_ref.at[0, :, there], P0.at[:, c]),
        (pol_ref.at[1, :, there], P1.at[:, c]),
        (mat_ref.at[there], mat.at[c]),
    ]
    swaps = [
        pltpu.make_async_remote_copy(
            src_ref=s, dst_ref=d, send_sem=swap_send.at[i], recv_sem=swap_recv.at[i],
            device_id=partner, device_id_type=MESH,
        )
        for i, (s, d) in enumerate(swaps)
    ]
    for copy in swaps:
        copy.start()

    def halos(p):
        def message(k, src, dst, device):
            return pltpu.make_async_remote_copy(
                src_ref=src, dst_ref=dst, send_sem=halo_send.at[k], recv_sem=halo_recv.at[p, k],
                device_id=device, device_id_type=MESH,
            )

        e = E[p]
        own, rows = pl.ds(1, HX), pl.ds(8, BY)
        along_x = [
            (has_up, has_down, message(0, e.at[:, :, HX, rows], e.at[:, :, 0, rows], up)),
            (has_down, has_up, message(1, e.at[1:3, :, 1, rows], e.at[1:3, :, HX + 1, rows], down)),
            (
                jnp.logical_and(has_up, has_left), jnp.logical_and(has_down, has_right),
                message(5, e.at[0, :, HX, 8:9], e.at[0, :, 0, 24:25], up_left),
            ),
            (
                jnp.logical_and(has_down, has_right), jnp.logical_and(has_up, has_left),
                message(6, e.at[1, :, 1, 23:24], e.at[1, :, HX + 1, 7:8], down_right),
            ),
        ]
        along_y = [
            (has_right, has_left, message(2, e.at[:, :, own, 23:24], e.at[:, :, own, 7:8], right)),
            (has_left, has_right, message(3, e.at[0, :, own, 8:9], e.at[0, :, own, 24:25], left)),
            (has_left, has_right, message(4, e.at[2, :, own, 8:9], e.at[2, :, own, 24:25], left)),
        ]
        return along_y, along_x

    def start(messages):
        for receiver, _, copy in messages:
            @pl.when(receiver)
            def _(copy=copy):
                copy.start()

    def finish(messages):
        for receiver, sender, copy in messages:
            @pl.when(sender)
            def _(copy=copy):
                copy.wait_recv()

            @pl.when(receiver)
            def _(copy=copy):
                copy.wait_send()

    def first(k, src, dst, device):
        return pltpu.make_async_remote_copy(
            src_ref=src, dst_ref=dst, send_sem=first_send.at[k], recv_sem=first_recv.at[k],
            device_id=device, device_id_type=MESH,
        )

    own, rows = pl.ds(1, HX), pl.ds(8, BY)
    h_layers = [
        (has_up, has_down, first(0, H.at[1:3, :, HX, rows], H.at[1:3, :, 0, rows], up)),
        (has_right, has_left, first(1, H.at[0, :, own, 23:24], H.at[0, :, own, 7:8], right)),
        (has_right, has_left, first(2, H.at[2, :, own, 23:24], H.at[2, :, own, 7:8], right)),
    ]
    along_y, along_x = halos(0)
    loads[0].wait()
    swaps[0].wait()
    start(along_x)
    start(along_y)
    loads[1].wait()
    swaps[1].wait()
    start(h_layers)
    for i in range(2, 5):
        loads[i].wait()
        swaps[i].wait()
    for copy in loads[5:]:
        copy.wait()

    rates = [[], [], [], []]
    for m in range(NMAT):
        turning = jnp.full((8, 128), freq_ref[m], F32) * DT
        half_loss = jnp.full((8, 128), damp_ref[m], F32) * (0.5 * DT)
        denominator = 1.0 + half_loss
        rates[0].append((2.0 - turning * turning) / denominator)
        rates[1].append(-(1.0 - half_loss) / denominator)
        rates[2].append(jnp.full((8, 128), strength_ref[m], F32) * turning * turning / denominator)
        rates[3].append(1.0 / jnp.full((8, 128), eps_ref[m], F32))

    @pl.loop(0, HX)
    def _(i):
        for z in range(2):
            for j in range(2):
                cell = mat[z, i, 8 * j:8 * j + 8]
                for k in range(4):
                    value = jnp.where(cell == 1, rates[k][1], rates[k][0])
                    value = jnp.where(cell == 2, rates[k][2], value)
                    coef[k, z, i, 8 * j:8 * j + 8] = jnp.where(cell == 3, rates[k][3], value)

    finish(h_layers)

    lane = lax.broadcasted_iota(jnp.int32, (8, 128), 1)
    last_lane, first_lane = lane == 127, lane == 0

    def ahead_z(v):
        r0, r1 = (pltpu.roll(x, 127, 1) for x in v)
        return jnp.where(last_lane, r1, r0), jnp.where(last_lane, 0.0, r1)

    def behind_z(v):
        r0, r1 = (pltpu.roll(x, 1, 1) for x in v)
        return jnp.where(first_lane, 0.0, r0), jnp.where(first_lane, r0, r1)

    def magnetic(e, i, j, keep=None):
        r = pl.ds(8 * j, 8)
        r1 = pl.ds(8 * j + 1, 8)
        ex, ey, ez = ([e[d, z, i, r] for z in range(2)] for d in range(3))
        ex_z, ey_z = ahead_z(ex), ahead_z(ey)
        for z in range(2):
            hx = H[0, z, i, r] - DT * ((e[2, z, i, r1] - ez[z]) - (ey_z[z] - ey[z]))
            hz = H[2, z, i, r] - DT * ((e[1, z, i + 1, r] - ey[z]) - (e[0, z, i, r1] - ex[z]))
            H[0, z, i, r] = hx if keep is None else jnp.where(keep, hx, 0.0)
            H[2, z, i, r] = hz if keep is None else jnp.where(keep, hz, 0.0)
            if j > 0:
                hy = H[1, z, i, r] - DT * ((ex_z[z] - ex[z]) - (e[2, z, i + 1, r] - ez[z]))
                H[1, z, i, r] = hy if keep is None else jnp.where(keep, hy, 0.0)

    def electric(e, e_new, now_ref, old_ref, i, j):
        r = pl.ds(8 * j, 8)
        r1 = pl.ds(8 * j - 1, 8)
        s = pl.ds(8 * (j - 1), 8)
        hx, hy, hz = ([H[d, z, i, r] for z in range(2)] for d in range(3))
        hx_z, hy_z = behind_z(hx), behind_z(hy)
        for z in range(2):
            curl = (
                (hz[z] - H[2, z, i, r1]) - (hy[z] - hy_z[z]),
                (hx[z] - hx_z[z]) - (hz[z] - H[2, z, i - 1, r]),
                (hy[z] - H[1, z, i - 1, r]) - (hx[z] - H[0, z, i, r1]),
            )
            keep, back, drive, inverse = (coef[k, z, i - 1, s] for k in range(4))
            for d in range(3):
                value = e[d, z, i, r]
                now = now_ref[d, z, i - 1, s]
                new = keep * now + back * old_ref[d, z, i - 1, s] + drive * value
                old_ref[d, z, i - 1, s] = new
                e_new[d, z, i, r] = value + inverse * (DT * curl[d] - (new - now))

    def sample_copy(n, k, g, t):
        return pltpu.make_async_remote_copy(
            src_ref=stage.at[n, t], dst_ref=samp.at[n], send_sem=samp_send.at[k], recv_sem=samp_recv.at[n],
            device_id=(g, gy, t), device_id_type=MESH,
        )

    def row_copies(n):
        return [
            sample_copy(n, 2 * k + t, row_end - 1 - lax.rem(k + 1, ROW - 1), t) for k in range(ROW - 1) for t in range(2)
        ] + [sample_copy(n, 2 * ROW - 2, row_end, 0)]

    def relay_copy(n, k):
        return pltpu.make_async_remote_copy(
            src_ref=stage.at[n], dst_ref=stage.at[n], send_sem=samp_send.at[2 * ROW - 1 + k],
            recv_sem=samp_recv.at[n], device_id=(ROW * k + ROW - 1, gy, 1), device_id_type=MESH,
        )

    def relay_copies(n):
        return [relay_copy(n, k) for k in range(NGX // ROW - 1)]

    def relay(n):
        @pl.when(is_relay)
        def _():
            @pl.when(n > 0)
            def _():
                for copy in row_copies(n - 1):
                    copy.wait_send()

            relay_copy(n, 0).wait_recv()
            for copy in row_copies(n):
                copy.start()
            samp[n] = stage[n, 1]

    def start_next(n, p):
        @pl.when(n < STEPS - 1)
        def _():
            along_y, along_x = halos(p)
            start(along_x)
            start(along_y)

    def step(n, p):
        e, e_new = E[p], E[1 - p]
        now_ref, old_ref = (P0, P1) if p == 0 else (P1, P0)

        along_y, along_x = halos(p)

        @pl.loop(0, 3)
        def _(b):
            for u in range(5):
                magnetic(e, 1 + 5 * b + u, 1)

        finish(along_y)

        @pl.loop(0, 3)
        def _(b):
            for u in range(5):
                magnetic(e, 1 + 5 * b + u, 0, has_left)
                magnetic(e, 1 + 5 * b + u, 2)

        @pl.loop(0, 2)
        def _(b):
            for u in range(7):
                electric(e, e_new, now_ref, old_ref, 2 + 7 * b + u, 1)
                electric(e, e_new, now_ref, old_ref, 2 + 7 * b + u, 2)

        finish(along_x)
        magnetic(e, 0, 1, has_down)
        magnetic(e, 0, 2, has_down)
        magnetic(e, HX, 0, has_left)
        for j in (1, 2):
            magnetic(e, HX, j)
        for i in (1, HX):
            for j in (1, 2):
                electric(e, e_new, now_ref, old_ref, i, j)

        start_next(n, 1 - p)

        @pl.when(n > 0)
        def _():
            relay(n - 1)

        @pl.when(is_holder)
        def _():
            @pl.when(n > 0)
            def _():
                for copy in relay_copies(n - 1) + row_copies(n - 1):
                    copy.wait_send()

            for t in range(2):
                for d in range(2):
                    stage[n, t, d] = e_new[d + 1, t, 1, 8:24]
                    stage[n, t, d + 2] = H[d + 1, t, 1, 8:24]
            for copy in relay_copies(n) + row_copies(n):
                copy.start()
            samp[n] = stage[n, 1]

    @pl.loop(0, STEPS // 2)
    def _(b):
        step(2 * b, 0)
        step(2 * b + 1, 1)

    e_out = lambda z: (E0.at[:, z, own, rows], out_f.at[0:3, here])
    h_out = lambda z: (H.at[:, z, own, rows], out_f.at[3:6, here])
    p_out = lambda z: (P0.at[:, z], out_p.at[0, :, here])
    q_out = lambda z: (P1.at[:, z], out_p.at[1, :, here])
    sends = []
    for k, out in enumerate((e_out, h_out, p_out, q_out)):
        s, d = out(other)
        sends.append(pltpu.make_async_remote_copy(
            src_ref=s, dst_ref=d, send_sem=out_send.at[k], recv_sem=out_recv.at[k],
            device_id=partner, device_id_type=MESH,
        ))
        s, d = out(c)
        sends.append(pltpu.make_async_copy(s, d, out_sem.at[k]))
    @pl.when(jnp.logical_not(is_relay))
    def _():
        for copy in sends:
            copy.start()

    last = STEPS - 1
    relay(last)

    @pl.when(is_relay)
    def _():
        for copy in sends:
            copy.start()

    is_end = jnp.logical_not(jnp.logical_or(is_holder, is_relay))

    @pl.when(is_end)
    def _():
        for n in range(last):
            sample_copy(n, 0, 0, 0).wait_recv()

    def sample(n):
        return samp[n].reshape(4 * BY, 128)

    def weight(n, f):
        return weight_ref[n, 2 * gx + f], weight_ref[n, NF + 2 * gx + f]

    for f in range(2):
        for k in range(2):
            total = weight(0, f)[k] * sample(0)
            for n in range(1, last):
                total += weight(n, f)[k] * sample(n)
            sums[f, 64 * k:64 * k + 64] = total

    mine = (owner_ref[...] == gx).astype(F32)
    row = lax.broadcasted_iota(jnp.int32, (64, 64), 0)
    col = lax.broadcasted_iota(jnp.int32, (64, 64), 1)
    rank = jnp.dot(
        jnp.broadcast_to(mine, (8, 64)), (row < col).astype(F32), precision=HIGHEST, preferred_element_type=F32
    )
    slot = lax.broadcasted_iota(jnp.int32, (8, 64), 0).astype(F32)
    picked = jnp.where(rank == slot, mine, 0.0)

    def choose(n):
        return jnp.dot(picked, sample(n), precision=HIGHEST, preferred_element_type=F32)

    chosen = [choose(n) for n in range(last)]
    for s in range(SLOTS):
        for k in range(2 * NF // 8):
            total = spread[0, 8 * k:8 * k + 8] * chosen[0][s:s + 1]
            for n in range(1, last):
                total += spread[n, 8 * k:8 * k + 8] * chosen[n][s:s + 1]
            out_s[0, 0, 0, s, 8 * k:8 * k + 8] = total

    @pl.when(is_end)
    def _():
        sample_copy(last, 0, 0, 0).wait_recv()

    for f in range(2):
        for k in range(2):
            sums[f, 64 * k:64 * k + 64] += weight(last, f)[k] * sample(last)
        inner = jnp.dot(sums[f], ztab[f], precision=HIGHEST, preferred_element_type=F32)
        inner_real = inner[:64, :128] - inner[64:, 128:]
        inner_imag = inner[:64, 128:] + inner[64:, :128]
        cos_y, sin_y = ytab[f, 0], ytab[f, 1]
        lines = []
        for d in range(4):
            re, im = inner_real[16 * d:16 * d + 16], inner_imag[16 * d:16 * d + 16]
            lines.append(jnp.sum(re * cos_y - im * sin_y, axis=0, keepdims=True))
            lines.append(jnp.sum(re * sin_y + im * cos_y, axis=0, keepdims=True))
        part[f] = jnp.concatenate(lines, axis=0)

    far = []
    for k in range(1, NGY * NAF):
        them = lax.rem(me + k, NGY * NAF)
        far.append(pltpu.make_async_remote_copy(
            src_ref=part.at[them // 4], dst_ref=parts.at[k], send_sem=far_send.at[k], recv_sem=far_recv.at[k],
            device_id=(gx, them // NAF, lax.rem(them, NAF)), device_id_type=MESH,
        ))
    for copy in far:
        copy.start()

    chosen = choose(last)
    for s in range(SLOTS):
        for k in range(2 * NF // 8):
            out_s[0, 0, 0, s, 8 * k:8 * k + 8] += spread[last, 8 * k:8 * k + 8] * chosen[s:s + 1]

    total = part[me // 4]
    for k in range(1, NGY * NAF):
        far[k - 1].wait()
        total += parts[k]
    block = lax.rem(me, 4)
    total = pltpu.roll(total, lax.rem(128 - 32 * block, 128), 1)
    out_far[...] = total[:, :32]
    for copy in sends:
        copy.wait()

    @pl.when(is_holder)
    def _():
        for copy in relay_copies(last) + row_copies(last):
            copy.wait_send()

    @pl.when(is_relay)
    def _():
        for copy in row_copies(last):
            copy.wait_send()


def write_out(*refs):
    count = len(refs) // 2
    sem = refs[-1]
    copies = [pltpu.make_async_copy(refs[i], refs[count + i], sem.at[i]) for i in range(count)]
    for copy in copies:
        copy.start()
    for copy in copies:
        copy.wait()


def on_device(constants, fields, polarization, material, eps_inf, pole_strength, pole_freq, damping, owner):
    weights, spread, z_table, y_table = constants
    smem = pl.BlockSpec(memory_space=pltpu.SMEM)
    vmem = pl.BlockSpec(memory_space=pltpu.VMEM)
    hbm = pl.BlockSpec(memory_space=pl.ANY)
    dma = lambda *shape: pltpu.SemaphoreType.DMA(shape)
    shapes = (fields.shape, polarization.shape, (1, 1, 1, SLOTS, 2 * NF, BZ), (8, 32))
    results = pl.pallas_call(
        kernel,
        out_shape=(
            *(pltpu.VMEM(shape, F32) for shape in shapes),
        ),
        in_specs=[smem] * 5 + [vmem] + [hbm] * 6,
        out_specs=(vmem, vmem, vmem, vmem),
        scratch_shapes=[
            pltpu.VMEM((3, 2, HX + 2, 32, 128), F32),
            pltpu.VMEM((3, 2, HX + 2, 32, 128), F32),
            pltpu.VMEM((3, 2, HX + 1, 24, 128), F32),
            pltpu.VMEM((3, 2, HX, BY, 128), F32),
            pltpu.VMEM((3, 2, HX, BY, 128), F32),
            pltpu.VMEM((2, HX, BY, 128), jnp.int32),
            pltpu.VMEM((4, 2, HX, BY, 128), F32),
            pltpu.VMEM((STEPS, 2, 4, BY, 128), F32),
            pltpu.VMEM((STEPS, 4, BY, 128), F32),
            pltpu.VMEM((2, BZ, 2 * NANG), F32),
            pltpu.VMEM((2, 2, BY, NANG), F32),
            pltpu.VMEM((STEPS, 2 * NF, 128), F32),
            pltpu.VMEM((2, 128, 128), F32),
            pltpu.VMEM((2, 8, 128), F32),
            pltpu.VMEM((8, 8, 128), F32),
            dma(8), dma(5), dma(5), dma(7), dma(2, 7), dma(3), dma(3),
            dma(2 * ROW + 2), dma(STEPS), dma(8), dma(8), dma(4), dma(4), dma(4),
        ],
        compiler_params=pltpu.CompilerParams(
            collective_id=0, has_side_effects=True, vmem_limit_bytes=56 << 20
        ),
        name="fdtd",
    )(
        eps_inf, pole_strength, pole_freq, damping, weights, owner.reshape(1, 64),
        fields, polarization, material, spread, z_table, y_table,
    )
    return pl.pallas_call(
        write_out,
        out_shape=tuple(jax.ShapeDtypeStruct(shape, F32) for shape in shapes),
        in_specs=[vmem] * 4,
        out_specs=[hbm] * 4,
        scratch_shapes=[dma(4)],
        name="write_out",
    )(*(pltpu.with_memory_space_constraint(x, pltpu.VMEM) for x in results))


def solution(mesh):
    constants = tables()

    def whole(*arguments):
        return on_device(tuple(jnp.asarray(x) for x in constants), *arguments)

    return jax.shard_map(
        whole,
        mesh=mesh,
        in_specs=(
            P(None, "gx", "gy", "af"),
            P(None, None, "gx", "gy", "af"),
            P("gx", "gy", "af"),
            P(), P(), P(), P(),
            P("gy", "af", None, None),
        ),
        out_specs=(
            P(None, "gx", "gy", "af"),
            P(None, None, "gx", "gy", "af"),
            P("gx", "gy", "af", None, None, None),
            P(None, ("gx", "gy", "af")),
        ),
        check_vma=False,
    )
```

```python
import functools
import math

import jax
import jax.numpy as jnp
import numpy as np
from jax import lax
from jax.experimental import pallas as pl
from jax.experimental.pallas import tpu as pltpu
from jax.sharding import PartitionSpec as P

STEPS = 8
NF = 32
NANG = 128
NMAT = 4
NGX, NGY, NAF = 16, 4, 2
BX, BY, BZ = 32, 16, 128
HX = BX // 2
ROW = 4
SLOTS = 8
DT = 0.5
MESH = pl.DeviceIdType.MESH
HIGHEST = lax.Precision.HIGHEST
F32 = jnp.float32


def tables():
    omega = 0.25 + 1.5 * np.arange(NF) / NF
    t = (np.arange(STEPS) + 1.0) * DT
    phase = t[:, None] * omega[None, :]
    weights = np.concatenate([np.cos(phase), -np.sin(phase)], axis=1) / STEPS
    angle = np.arange(NANG)
    rho = 0.25 + 0.7 * (angle + 0.5) / NANG
    s_y = rho * np.cos(2.0 * np.pi * angle / NANG)
    s_z = rho * np.sin(2.0 * np.pi * angle / NANG)
    z_phase = omega[:, None, None] * s_z[None, None, :] * np.arange(BZ)[None, :, None]
    z_table = np.concatenate([np.cos(z_phase), np.sin(z_phase)], axis=2)
    z_table = z_table.reshape(NGX, 2, BZ, 2 * NANG)
    y = np.arange(NGY * BY).reshape(NGY, 1, BY)
    z0 = (BZ * np.arange(NAF)).reshape(1, NAF, 1)
    shift = s_y * y[..., None] + s_z * z0[..., None]
    y_phase = omega[:, None, None] * shift[:, :, None]
    y_table = np.stack([np.cos(y_phase), np.sin(y_phase)], axis=3)
    y_table = y_table / math.sqrt(NGY * BY * NAF * BZ)
    y_table = y_table.reshape(NGY * NAF, NGX, 2, 2, BY, NANG)
    spread = np.broadcast_to(weights[:, :, None], (STEPS, 2 * NF, 128))
    return (
        weights.astype(np.float32),
        spread.astype(np.float32),
        z_table.astype(np.float32),
        y_table.astype(np.float32),
    )


def kernel(
    eps_ref, strength_ref, freq_ref, damp_ref, weight_ref, owner_ref,
    fields_ref, pol_ref, mat_ref, spread_hbm, ztab_hbm, ytab_hbm,
    out_f, out_p, out_s, out_far,
    E0, E1, H, P0, P1, mat, coef, stage, samp, ztab, ytab, spread, sums, part, parts,
    local_sem, swap_send, swap_recv, halo_send, halo_recv, first_send, first_recv,
    samp_send, samp_recv, far_send, far_recv, out_sem, out_send, out_recv,
):
    gx, gy, c = lax.axis_index("gx"), lax.axis_index("gy"), lax.axis_index("af")
    half = lax.rem(gx + c + 1, 2)
    place = 2 * gx + half
    E = (E0, E1)
    other = 1 - c
    has_up, has_down = place < 2 * NGX - 1, place > 0
    has_right, has_left = gy < NGY - 1, gy > 0
    up_core = jnp.where(half == 1, c, other)
    down_core = jnp.where(half == 1, other, c)
    up = (gx + half, gy, up_core)
    down = (gx - (1 - half), gy, down_core)
    right, left = (gx, gy + 1, c), (gx, gy - 1, c)
    up_left = (gx + half, gy - 1, up_core)
    down_right = (gx - (1 - half), gy + 1, down_core)
    partner = (gx, gy, other)
    is_holder = jnp.logical_and(gx == NGX - 1, c == 1)
    row_end = gx // ROW * ROW + ROW - 1
    is_last_row = gx // ROW == NGX // ROW - 1
    is_relay = jnp.logical_and(jnp.logical_and(gx == row_end, c == 1), jnp.logical_not(is_last_row))
    fed_by_relay = jnp.logical_and(gx != row_end, jnp.logical_not(is_last_row))
    fed_by_holder = jnp.logical_or(is_relay, jnp.logical_and(is_last_row, gx != row_end))
    me = gy * NAF + c

    barrier = pltpu.get_barrier_semaphore()

    def greet(device):
        pl.semaphore_signal(barrier, inc=1, device_id=device, device_id_type=MESH)

    for k in range(1, NGY * NAF):
        them = lax.rem(me + k, NGY * NAF)
        greet((gx, them // NAF, lax.rem(them, NAF)))
    across_up = jnp.logical_and(half == 1, has_up)
    across_down = jnp.logical_and(half == 0, has_down)
    across_up_left = jnp.logical_and(across_up, has_left)
    across_down_right = jnp.logical_and(across_down, has_right)
    for there, device in (
        (across_up, up), (across_down, down), (across_up_left, up_left), (across_down_right, down_right),
    ):
        @pl.when(there)
        def _(device=device):
            greet(device)

    @pl.when(fed_by_relay)
    def _():
        greet((row_end, gy, 1))

    @pl.when(fed_by_holder)
    def _():
        greet((NGX - 1, gy, 1))

    here = pl.ds(half * HX, HX)
    there = pl.ds((1 - half) * HX, HX)
    loads = [
        (fields_ref.at[0:3, here], E0.at[:, c, 1:HX + 1, 8:24]),
        (fields_ref.at[3:6, here], H.at[:, c, 1:HX + 1, 8:24]),
        (pol_ref.at[0, :, here], P0.at[:, c]),
        (pol_ref.at[1, :, here], P1.at[:, c]),
        (mat_ref.at[here], mat.at[c]),
        (ztab_hbm.at[gx], ztab),
        (ytab_hbm.at[me, gx], ytab),
        (spread_hbm, spread),
    ]
    loads = [pltpu.make_async_copy(s, d, local_sem.at[i]) for i, (s, d) in enumerate(loads)]
    for copy in loads:
        copy.start()

    @pl.when(jnp.logical_not(has_up))
    def _():
        for p in range(2):
            for d in (1, 2):
                for z in range(2):
                    E[p][d, z, HX + 1, 0:24] = jnp.zeros((24, 128), F32)

    @pl.when(jnp.logical_not(has_right))
    def _():
        @pl.loop(0, HX + 1)
        def _(i):
            for p in range(2):
                for d in (0, 2):
                    for z in range(2):
                        E[p][d, z, i, 24:32] = jnp.zeros((8, 128), F32)

    count = (
        NGY * NAF - 1
        + across_up.astype(jnp.int32) + across_down.astype(jnp.int32)
        + across_up_left.astype(jnp.int32) + across_down_right.astype(jnp.int32)
        + jnp.where(is_holder, NGX // ROW - 1 + 2 * (ROW - 1), 0)
        + jnp.where(is_relay, 2 * (ROW - 1), 0)
    )
    pl.semaphore_wait(barrier, count)

    swaps = [
        (fields_ref.at[0:3, there], E0.at[:, c, 1:HX + 1, 8:24]),
        (fields_ref.at[3:6, there], H.at[:, c, 1:HX + 1, 8:24]),
        (pol_ref.at[0, :, there], P0.at[:, c]),
        (pol_ref.at[1, :, there], P1.at[:, c]),
        (mat_ref.at[there], mat.at[c]),
    ]
    swaps = [
        pltpu.make_async_remote_copy(
            src_ref=s, dst_ref=d, send_sem=swap_send.at[i], recv_sem=swap_recv.at[i],
            device_id=partner, device_id_type=MESH,
        )
        for i, (s, d) in enumerate(swaps)
    ]
    for copy in swaps:
        copy.start()

    def halos(p):
        def message(k, src, dst, device):
            return pltpu.make_async_remote_copy(
                src_ref=src, dst_ref=dst, send_sem=halo_send.at[k], recv_sem=halo_recv.at[p, k],
                device_id=device, device_id_type=MESH,
            )

        e = E[p]
        own, rows = pl.ds(1, HX), pl.ds(8, BY)
        along_x = [
            (has_up, has_down, message(0, e.at[:, :, HX, rows], e.at[:, :, 0, rows], up)),
            (has_down, has_up, message(1, e.at[1:3, :, 1, rows], e.at[1:3, :, HX + 1, rows], down)),
            (
                jnp.logical_and(has_up, has_left), jnp.logical_and(has_down, has_right),
                message(5, e.at[0, :, HX, 8:9], e.at[0, :, 0, 24:25], up_left),
            ),
            (
                jnp.logical_and(has_down, has_right), jnp.logical_and(has_up, has_left),
                message(6, e.at[1, :, 1, 23:24], e.at[1, :, HX + 1, 7:8], down_right),
            ),
        ]
        along_y = [
            (has_right, has_left, message(2, e.at[:, :, own, 23:24], e.at[:, :, own, 7:8], right)),
            (has_left, has_right, message(3, e.at[0, :, own, 8:9], e.at[0, :, own, 24:25], left)),
            (has_left, has_right, message(4, e.at[2, :, own, 8:9], e.at[2, :, own, 24:25], left)),
        ]
        return along_y, along_x

    def start(messages):
        for receiver, _, copy in messages:
            @pl.when(receiver)
            def _(copy=copy):
                copy.start()

    def finish(messages):
        for receiver, sender, copy in messages:
            @pl.when(sender)
            def _(copy=copy):
                copy.wait_recv()

            @pl.when(receiver)
            def _(copy=copy):
                copy.wait_send()

    def first(k, src, dst, device):
        return pltpu.make_async_remote_copy(
            src_ref=src, dst_ref=dst, send_sem=first_send.at[k], recv_sem=first_recv.at[k],
            device_id=device, device_id_type=MESH,
        )

    own, rows = pl.ds(1, HX), pl.ds(8, BY)
    h_layers = [
        (has_up, has_down, first(0, H.at[1:3, :, HX, rows], H.at[1:3, :, 0, rows], up)),
        (has_right, has_left, first(1, H.at[0, :, own, 23:24], H.at[0, :, own, 7:8], right)),
        (has_right, has_left, first(2, H.at[2, :, own, 23:24], H.at[2, :, own, 7:8], right)),
    ]
    along_y, along_x = halos(0)
    loads[0].wait()
    swaps[0].wait()
    start(along_x)
    start(along_y)
    loads[1].wait()
    swaps[1].wait()
    start(h_layers)
    for i in range(2, 5):
        loads[i].wait()
        swaps[i].wait()
    for copy in loads[5:]:
        copy.wait()

    rates = [[], [], [], []]
    for m in range(NMAT):
        turning = jnp.full((8, 128), freq_ref[m], F32) * DT
        half_loss = jnp.full((8, 128), damp_ref[m], F32) * (0.5 * DT)
        denominator = 1.0 + half_loss
        rates[0].append((2.0 - turning * turning) / denominator)
        rates[1].append(-(1.0 - half_loss) / denominator)
        rates[2].append(jnp.full((8, 128), strength_ref[m], F32) * turning * turning / denominator)
        rates[3].append(1.0 / jnp.full((8, 128), eps_ref[m], F32))

    @pl.loop(0, HX)
    def _(i):
        for z in range(2):
            for j in range(2):
                cell = mat[z, i, 8 * j:8 * j + 8]
                for k in range(4):
                    value = jnp.where(cell == 1, rates[k][1], rates[k][0])
                    value = jnp.where(cell == 2, rates[k][2], value)
                    coef[k, z, i, 8 * j:8 * j + 8] = jnp.where(cell == 3, rates[k][3], value)

    finish(h_layers)

    lane = lax.broadcasted_iota(jnp.int32, (8, 128), 1)
    last_lane, first_lane = lane == 127, lane == 0

    def ahead_z(v):
        r0, r1 = (pltpu.roll(x, 127, 1) for x in v)
        return jnp.where(last_lane, r1, r0), jnp.where(last_lane, 0.0, r1)

    def behind_z(v):
        r0, r1 = (pltpu.roll(x, 1, 1) for x in v)
        return jnp.where(first_lane, 0.0, r0), jnp.where(first_lane, r0, r1)

    def magnetic(e, i, j, keep=None):
        r = pl.ds(8 * j, 8)
        r1 = pl.ds(8 * j + 1, 8)
        ex, ey, ez = ([e[d, z, i, r] for z in range(2)] for d in range(3))
        ex_z, ey_z = ahead_z(ex), ahead_z(ey)
        for z in range(2):
            hx = H[0, z, i, r] - DT * ((e[2, z, i, r1] - ez[z]) - (ey_z[z] - ey[z]))
            hz = H[2, z, i, r] - DT * ((e[1, z, i + 1, r] - ey[z]) - (e[0, z, i, r1] - ex[z]))
            H[0, z, i, r] = hx if keep is None else jnp.where(keep, hx, 0.0)
            H[2, z, i, r] = hz if keep is None else jnp.where(keep, hz, 0.0)
            if j > 0:
                hy = H[1, z, i, r] - DT * ((ex_z[z] - ex[z]) - (e[2, z, i + 1, r] - ez[z]))
                H[1, z, i, r] = hy if keep is None else jnp.where(keep, hy, 0.0)

    def electric(e, e_new, now_ref, old_ref, i, j):
        r = pl.ds(8 * j, 8)
        r1 = pl.ds(8 * j - 1, 8)
        s = pl.ds(8 * (j - 1), 8)
        hx, hy, hz = ([H[d, z, i, r] for z in range(2)] for d in range(3))
        hx_z, hy_z = behind_z(hx), behind_z(hy)
        for z in range(2):
            curl = (
                (hz[z] - H[2, z, i, r1]) - (hy[z] - hy_z[z]),
                (hx[z] - hx_z[z]) - (hz[z] - H[2, z, i - 1, r]),
                (hy[z] - H[1, z, i - 1, r]) - (hx[z] - H[0, z, i, r1]),
            )
            keep, back, drive, inverse = (coef[k, z, i - 1, s] for k in range(4))
            for d in range(3):
                value = e[d, z, i, r]
                now = now_ref[d, z, i - 1, s]
                new = keep * now + back * old_ref[d, z, i - 1, s] + drive * value
                old_ref[d, z, i - 1, s] = new
                e_new[d, z, i, r] = value + inverse * (DT * curl[d] - (new - now))

    def sample_copy(n, k, g, t):
        return pltpu.make_async_remote_copy(
            src_ref=stage.at[n, t], dst_ref=samp.at[n], send_sem=samp_send.at[k], recv_sem=samp_recv.at[n],
            device_id=(g, gy, t), device_id_type=MESH,
        )

    def row_copies(n):
        return [
            sample_copy(n, 2 * k + t, row_end - ROW + 1 + k, t) for k in range(ROW - 1) for t in range(2)
        ] + [sample_copy(n, 2 * ROW - 2, row_end, 0)]

    def relay_copy(n, k):
        return pltpu.make_async_remote_copy(
            src_ref=stage.at[n], dst_ref=stage.at[n], send_sem=samp_send.at[2 * ROW - 1 + k],
            recv_sem=samp_recv.at[n], device_id=(ROW * k + ROW - 1, gy, 1), device_id_type=MESH,
        )

    def relay_copies(n):
        return [relay_copy(n, k) for k in range(NGX // ROW - 1)]

    def relay(n):
        @pl.when(is_relay)
        def _():
            @pl.when(n > 0)
            def _():
                for copy in row_copies(n - 1):
                    copy.wait_send()

            relay_copy(n, 0).wait_recv()
            for copy in row_copies(n):
                copy.start()
            samp[n] = stage[n, 1]

    def start_next(n, p):
        @pl.when(n < STEPS - 1)
        def _():
            along_y, along_x = halos(p)
            start(along_x)
            start(along_y)

    def step(n, p):
        e, e_new = E[p], E[1 - p]
        now_ref, old_ref = (P0, P1) if p == 0 else (P1, P0)

        along_y, along_x = halos(p)

        @pl.loop(0, 3)
        def _(b):
            for u in range(5):
                magnetic(e, 1 + 5 * b + u, 1)

        finish(along_y)

        for i in range(1, HX):
            magnetic(e, i, 0, has_left)
            magnetic(e, i, 2)
        for i in range(2, HX):
            electric(e, e_new, now_ref, old_ref, i, 1)
            electric(e, e_new, now_ref, old_ref, i, 2)

        finish(along_x)
        magnetic(e, 0, 1, has_down)
        magnetic(e, 0, 2, has_down)
        magnetic(e, HX, 0, has_left)
        for j in (1, 2):
            magnetic(e, HX, j)
        for i in (1, HX):
            for j in (1, 2):
                electric(e, e_new, now_ref, old_ref, i, j)

        start_next(n, 1 - p)

        @pl.when(n > 0)
        def _():
            relay(n - 1)

        @pl.when(is_holder)
        def _():
            @pl.when(n > 0)
            def _():
                for copy in relay_copies(n - 1) + row_copies(n - 1):
                    copy.wait_send()

            for t in range(2):
                for d in range(2):
                    stage[n, t, d] = e_new[d + 1, t, 1, 8:24]
                    stage[n, t, d + 2] = H[d + 1, t, 1, 8:24]
            for copy in relay_copies(n) + row_copies(n):
                copy.start()
            samp[n] = stage[n, 1]

    @pl.loop(0, STEPS // 2)
    def _(b):
        step(2 * b, 0)
        step(2 * b + 1, 1)

    e_out = lambda z: (E0.at[:, z, own, rows], out_f.at[0:3, here])
    h_out = lambda z: (H.at[:, z, own, rows], out_f.at[3:6, here])
    p_out = lambda z: (P0.at[:, z], out_p.at[0, :, here])
    q_out = lambda z: (P1.at[:, z], out_p.at[1, :, here])
    sends = []
    for k, out in enumerate((e_out, h_out, p_out, q_out)):
        s, d = out(other)
        sends.append(pltpu.make_async_remote_copy(
            src_ref=s, dst_ref=d, send_sem=out_send.at[k], recv_sem=out_recv.at[k],
            device_id=partner, device_id_type=MESH,
        ))
        s, d = out(c)
        sends.append(pltpu.make_async_copy(s, d, out_sem.at[k]))
    @pl.when(jnp.logical_not(is_relay))
    def _():
        for copy in sends:
            copy.start()

    last = STEPS - 1
    relay(last)

    @pl.when(is_relay)
    def _():
        for copy in sends:
            copy.start()

    is_end = jnp.logical_not(jnp.logical_or(is_holder, is_relay))

    @pl.when(is_end)
    def _():
        for n in range(last):
            sample_copy(n, 0, 0, 0).wait_recv()

    def sample(n):
        return samp[n].reshape(4 * BY, 128)

    def weight(n, f):
        return weight_ref[n, 2 * gx + f], weight_ref[n, NF + 2 * gx + f]

    for f in range(2):
        for k in range(2):
            total = weight(0, f)[k] * sample(0)
            for n in range(1, last):
                total += weight(n, f)[k] * sample(n)
            sums[f, 64 * k:64 * k + 64] = total

    mine = (owner_ref[...] == gx).astype(F32)
    row = lax.broadcasted_iota(jnp.int32, (64, 64), 0)
    col = lax.broadcasted_iota(jnp.int32, (64, 64), 1)
    rank = jnp.dot(
        jnp.broadcast_to(mine, (8, 64)), (row < col).astype(F32), precision=HIGHEST, preferred_element_type=F32
    )
    slot = lax.broadcasted_iota(jnp.int32, (8, 64), 0).astype(F32)
    picked = jnp.where(rank == slot, mine, 0.0)

    def choose(n):
        return jnp.dot(picked, sample(n), precision=HIGHEST, preferred_element_type=F32)

    chosen = [choose(n) for n in range(last)]
    for s in range(SLOTS):
        for k in range(2 * NF // 8):
            total = spread[0, 8 * k:8 * k + 8] * chosen[0][s:s + 1]
            for n in range(1, last):
                total += spread[n, 8 * k:8 * k + 8] * chosen[n][s:s + 1]
            out_s[0, 0, 0, s, 8 * k:8 * k + 8] = total

    @pl.when(is_end)
    def _():
        sample_copy(last, 0, 0, 0).wait_recv()

    for f in range(2):
        for k in range(2):
            sums[f, 64 * k:64 * k + 64] += weight(last, f)[k] * sample(last)
        inner = jnp.dot(sums[f], ztab[f], precision=HIGHEST, preferred_element_type=F32)
        inner_real = inner[:64, :128] - inner[64:, 128:]
        inner_imag = inner[:64, 128:] + inner[64:, :128]
        cos_y, sin_y = ytab[f, 0], ytab[f, 1]
        lines = []
        for d in range(4):
            re, im = inner_real[16 * d:16 * d + 16], inner_imag[16 * d:16 * d + 16]
            lines.append(jnp.sum(re * cos_y - im * sin_y, axis=0, keepdims=True))
            lines.append(jnp.sum(re * sin_y + im * cos_y, axis=0, keepdims=True))
        part[f] = jnp.concatenate(lines, axis=0)

    far = []
    for k in range(1, NGY * NAF):
        them = lax.rem(me + k, NGY * NAF)
        far.append(pltpu.make_async_remote_copy(
            src_ref=part.at[them // 4], dst_ref=parts.at[k], send_sem=far_send.at[k], recv_sem=far_recv.at[k],
            device_id=(gx, them // NAF, lax.rem(them, NAF)), device_id_type=MESH,
        ))
    for copy in far:
        copy.start()

    chosen = choose(last)
    for s in range(SLOTS):
        for k in range(2 * NF // 8):
            out_s[0, 0, 0, s, 8 * k:8 * k + 8] += spread[last, 8 * k:8 * k + 8] * chosen[s:s + 1]

    total = part[me // 4]
    for k in range(1, NGY * NAF):
        far[k - 1].wait()
        total += parts[k]
    block = lax.rem(me, 4)
    total = pltpu.roll(total, lax.rem(128 - 32 * block, 128), 1)
    out_far[...] = total[:, :32]
    for copy in sends:
        copy.wait()

    @pl.when(is_holder)
    def _():
        for copy in relay_copies(last) + row_copies(last):
            copy.wait_send()

    @pl.when(is_relay)
    def _():
        for copy in row_copies(last):
            copy.wait_send()


def write_out(*refs):
    count = len(refs) // 2
    sem = refs[-1]
    copies = [pltpu.make_async_copy(refs[i], refs[count + i], sem.at[i]) for i in range(count)]
    for copy in copies:
        copy.start()
    for copy in copies:
        copy.wait()


def on_device(constants, fields, polarization, material, eps_inf, pole_strength, pole_freq, damping, owner):
    weights, spread, z_table, y_table = constants
    smem = pl.BlockSpec(memory_space=pltpu.SMEM)
    vmem = pl.BlockSpec(memory_space=pltpu.VMEM)
    hbm = pl.BlockSpec(memory_space=pl.ANY)
    dma = lambda *shape: pltpu.SemaphoreType.DMA(shape)
    shapes = (fields.shape, polarization.shape, (1, 1, 1, SLOTS, 2 * NF, BZ), (8, 32))
    results = pl.pallas_call(
        kernel,
        out_shape=(
            *(pltpu.VMEM(shape, F32) for shape in shapes),
        ),
        in_specs=[smem] * 5 + [vmem] + [hbm] * 6,
        out_specs=(vmem, vmem, vmem, vmem),
        scratch_shapes=[
            pltpu.VMEM((3, 2, HX + 2, 32, 128), F32),
            pltpu.VMEM((3, 2, HX + 2, 32, 128), F32),
            pltpu.VMEM((3, 2, HX + 1, 24, 128), F32),
            pltpu.VMEM((3, 2, HX, BY, 128), F32),
            pltpu.VMEM((3, 2, HX, BY, 128), F32),
            pltpu.VMEM((2, HX, BY, 128), jnp.int32),
            pltpu.VMEM((4, 2, HX, BY, 128), F32),
            pltpu.VMEM((STEPS, 2, 4, BY, 128), F32),
            pltpu.VMEM((STEPS, 4, BY, 128), F32),
            pltpu.VMEM((2, BZ, 2 * NANG), F32),
            pltpu.VMEM((2, 2, BY, NANG), F32),
            pltpu.VMEM((STEPS, 2 * NF, 128), F32),
            pltpu.VMEM((2, 128, 128), F32),
            pltpu.VMEM((2, 8, 128), F32),
            pltpu.VMEM((8, 8, 128), F32),
            dma(8), dma(5), dma(5), dma(7), dma(2, 7), dma(3), dma(3),
            dma(2 * ROW + 2), dma(STEPS), dma(8), dma(8), dma(4), dma(4), dma(4),
        ],
        compiler_params=pltpu.CompilerParams(
            collective_id=0, has_side_effects=True, vmem_limit_bytes=56 << 20
        ),
        name="fdtd",
    )(
        eps_inf, pole_strength, pole_freq, damping, weights, owner.reshape(1, 64),
        fields, polarization, material, spread, z_table, y_table,
    )
    return pl.pallas_call(
        write_out,
        out_shape=tuple(jax.ShapeDtypeStruct(shape, F32) for shape in shapes),
        in_specs=[vmem] * 4,
        out_specs=[hbm] * 4,
        scratch_shapes=[dma(4)],
        name="write_out",
    )(*(pltpu.with_memory_space_constraint(x, pltpu.VMEM) for x in results))


def solution(mesh):
    constants = tables()

    def whole(*arguments):
        return on_device(tuple(jnp.asarray(x) for x in constants), *arguments)

    return jax.shard_map(
        whole,
        mesh=mesh,
        in_specs=(
            P(None, "gx", "gy", "af"),
            P(None, None, "gx", "gy", "af"),
            P("gx", "gy", "af"),
            P(), P(), P(), P(),
            P("gy", "af", None, None),
        ),
        out_specs=(
            P(None, "gx", "gy", "af"),
            P(None, None, "gx", "gy", "af"),
            P("gx", "gy", "af", None, None, None),
            P(None, ("gx", "gy", "af")),
        ),
        check_vma=False,
    )
```
